32 devices in a mesh: loop: 16 (over z, x, core), bcast: 2 (over y).
Axes of the slice: x: 2, y: 2, z: 4, core: 2. Of those that a mesh axis runs over, the one named last changes fastest.
Arguments:
- s_blocks: float32 [16, 2, 2, 10, 256, 256], P('loop', 'bcast'), may hold values from -6 to 6
- s_list: int32 [16, 2, 2, 10, 2], P('loop', 'bcast'), may hold values from 0 to 3, as said below
- x_blocks: float32 [16, 2, 12, 256, 256], P('loop', 'bcast'), may hold values from -0.09375 to 0.09375
- x_list: int32 [16, 2, 12, 2], P('loop', 'bcast'), may hold values from 0 to 4, as said below
- c_list: int32 [16, 2, 10, 2], P('loop', 'bcast'), may hold values from 0 to 3, as said below
- owner: int32 [16, 4], P('loop'), may hold values from 0 to 1, as said below
Outputs:
- product: float32 [16, 2, 10, 256, 256], P('loop', 'bcast')
The draws below stay inside these ranges and needn't reach their ends.
Inputs may be any that keep to these rules, and one draw needn't show every extreme that they name: `s_list`: positions within one list are distinct. `x_list`: positions within one list are distinct; entries with first value 4 are empty and stand after the occupied ones; some device's list has no empty entry. `c_list`: positions within one list are distinct. owner[l, s] = (s + q_l) mod 2 for a whole number q_l of each block-row group.
All inputs are finite; a program needn't handle non-finite values.
Results may differ from the reference program's by a relative error of at most 0.0003.
Values sent between devices are 32-bit elements; how exact they have to be, the bound alone decides.
No kernel may reach another device: no remote copies, remote signals or barrier semaphores. Data moves between devices by JAX's collectives and lax.ppermute only.
A program may use at most 192 MiB of HBM per device.

```python
import jax
import jax.numpy as jnp
from jax import lax

BS = 256
RB = 3
KB = 4
CB = 4
STEPS = 4
SLOT_S = 10
SLOT_X = 12
SLOT_C = 10
STEP_DEV = 2
N_LOOP = 16
N_BCAST = 2


def draw_s_list(key, part):
    count = N_LOOP * N_BCAST * STEP_DEV
    keys = jax.random.split(jax.random.fold_in(key, 11), count)
    cells = jax.vmap(lambda one_key: jax.random.permutation(one_key, RB * KB)[:SLOT_S])(keys)
    placed = jnp.stack([cells // KB, cells % KB], -1).astype(jnp.int32)
    return placed.reshape((N_LOOP, N_BCAST, STEP_DEV, SLOT_S, 2))


def draw_x_list(key, part):
    count = N_LOOP * N_BCAST
    keys = jax.random.split(jax.random.fold_in(key, 23), count)
    cells = jax.vmap(lambda one_key: jax.random.permutation(one_key, KB * CB)[:SLOT_X])(keys)
    filled = jax.random.randint(jax.random.fold_in(key, 29), (count,), SLOT_X // 3, SLOT_X + 1)
    filled = filled.at[0].set(SLOT_X).at[1].set(SLOT_X // 3)
    used = jnp.arange(SLOT_X)[None, :] < filled[:, None]
    first = jnp.where(used, cells // CB, KB)
    placed = jnp.stack([first, cells % CB], -1).astype(jnp.int32)
    return placed.reshape((N_LOOP, N_BCAST, SLOT_X, 2))


def draw_c_list(key, part):
    count = N_LOOP * N_BCAST
    keys = jax.random.split(jax.random.fold_in(key, 37), count)
    cells = jax.vmap(lambda one_key: jax.random.permutation(one_key, RB * CB)[:SLOT_C])(keys)
    placed = jnp.stack([cells // CB, cells % CB], -1).astype(jnp.int32)
    return placed.reshape((N_LOOP, N_BCAST, SLOT_C, 2))


def draw_owner(key, part):
    rotate = jax.random.randint(jax.random.fold_in(key, 41), (N_LOOP,), 0, N_BCAST)
    rotate = rotate.at[0].set(N_BCAST - 1)
    return ((jnp.arange(STEPS)[None, :] + rotate[:, None]) % N_BCAST).astype(jnp.int32)


def levels(key, shape, shards, least, top_value):
    def one(axis_at, blocks):
        draws = jax.random.uniform(jax.random.fold_in(jax.random.fold_in(key, 6), axis_at), (blocks,), jnp.float32, least / len(shards), top_value / len(shards))
        return jnp.repeat(jnp.exp(draws), shape[axis_at] // blocks).reshape((-1,) + (1,) * (len(shape) - axis_at - 1))

    loudness = one(*shards[0])
    for cut in shards[1:]:
        loudness = loudness * one(*cut)
    return loudness


def normal_values(rng, shape, spread, limit, pieces=(), dtype=jnp.bfloat16):
    drawn = jax.random.normal(rng, shape, jnp.float32) * spread
    if len(pieces) > 0:
        drawn = levels(rng, shape, pieces, -0.22, 0.18) * drawn
    return jnp.clip(drawn, min=-limit, max=limit).astype(dtype)


def setup_inputs(seed: int = 0) -> dict:
    key_list = jax.random.split(jax.random.key(seed), 7)
    return {
        "s_blocks": normal_values(key_list[0], (N_LOOP, N_BCAST, STEP_DEV, SLOT_S, BS, BS), 1.0, 6.0, ((0, 16), (1, 2)), jnp.float32),
        "s_list": draw_s_list(jax.random.fold_in(key_list[6], 71), 0),
        "x_blocks": normal_values(key_list[2], (N_LOOP, N_BCAST, SLOT_X, BS, BS), (BS * KB * STEPS) ** -0.5, 0.09375, ((0, 16), (1, 2)), jnp.float32),
        "x_list": draw_x_list(jax.random.fold_in(key_list[6], 71), 0),
        "c_list": draw_c_list(jax.random.fold_in(key_list[6], 71), 0),
        "owner": draw_owner(jax.random.fold_in(key_list[6], 71), 0),
    }


HIGHEST = lax.Precision.HIGHEST


def densify(blocks, places, row_count, col_count):
    chosen = (places[:, 0][:, None, None] == jnp.arange(row_count)[None, :, None]) & (places[:, 1][:, None, None] == jnp.arange(col_count)[None, None, :])
    return jnp.einsum("irc,iab->rcab", chosen.astype(jnp.float32), blocks, precision=HIGHEST)


def retained(left, right, pairs):
    picked_left = left[pairs[:, 0]]
    picked_right = jnp.moveaxis(right[:, pairs[:, 1]], 1, 0)
    return jnp.einsum("jkab,jkbd->jad", picked_left, picked_right, precision=HIGHEST)


def reference(s_blocks, s_list, x_blocks, x_list, c_list, owner):
    def one_row(line):
        def one_device(column):
            total = jnp.zeros((SLOT_C, BS, BS), jnp.float32)
            pairs = c_list[line, column]
            for step in range(STEPS):
                root = owner[line, step]
                slot = step // N_BCAST
                left = densify(s_blocks[line, root, slot], s_list[line, root, slot], RB, KB)
                source = (line + step) % N_LOOP
                right = densify(x_blocks[source, column], x_list[source, column], KB, CB)
                total = total + retained(left, right, pairs)
            return total
        return lax.map(one_device, jnp.arange(N_BCAST))
    return lax.map(one_row, jnp.arange(N_LOOP))
```

```python
import functools

import jax
import jax.numpy as jnp
from jax import lax
from jax.experimental import pallas as pl
from jax.experimental.pallas import tpu as pltpu
from jax.sharding import PartitionSpec as P

RB = 3
KB = 4
CB = 4
STEPS = 4

X_AT = 0
OWN_FLAG_AT = X_AT + STEPS * KB * CB
GROUP_STEP_AT = OWN_FLAG_AT + STEPS
OUT_AT = GROUP_STEP_AT + STEPS


def positions(places, row_count, col_count):
    cells = jnp.arange(row_count * col_count)
    rows, cols = cells // col_count, cells % col_count
    there = (places[..., None, :, 0] == rows[:, None]) & (places[..., None, :, 1] == cols[:, None])
    return jnp.max(jnp.where(there, jnp.arange(places.shape[-2]), -1), axis=-1)


def halves(values):
    high = values.astype(jnp.bfloat16)
    return high, (values - high.astype(jnp.float32)).astype(jnp.bfloat16)


def dot(left, right):
    return jnp.dot(left, right, preferred_element_type=jnp.float32)


def product_terms(left_blocks, right_high, right_low):
    left_high, left_low = halves(jnp.concatenate(left_blocks, axis=0))
    return dot(left_high, right_high) + dot(left_high, right_low) + dot(left_low, right_high)


def group_kernel(group, own_at, first, n_own, meta, *refs):
    refs = list(refs)
    x_refs = [refs.pop(0) for _ in range(CB)]
    s_refs = [refs.pop(0) for _ in range(RB if n_own else 0)]
    if not first:
        acc_in = refs.pop(0)
        refs.pop(0)
    acc_ref, r_ref = refs
    k = pl.program_id(0)
    step = meta[GROUP_STEP_AT + group]

    @pl.when(k == 0)
    def _():
        acc_ref[...] = jnp.zeros_like(acc_ref) if first else acc_in[...]

    bs = x_refs[0].shape[-1]
    for c in range(CB):
        there = meta[X_AT + (step * KB + k) * CB + c] >= 0
        high, low = halves(jnp.where(there, x_refs[c][0], 0.0))
        r_ref[0, 0, :, c * bs : (c + 1) * bs] = high
        r_ref[0, 1, :, c * bs : (c + 1) * bs] = low

    if n_own:

        @pl.when(meta[OWN_FLAG_AT + step] > 0)
        def _():
            blocks = []
            for r in range(RB):
                there = meta[own_at + (step // 2) * RB * KB + r * KB + k] >= 0
                blocks.append(jnp.where(there, s_refs[r][0, 0], 0.0))
            terms = product_terms(blocks, r_ref[0, 0], r_ref[0, 1])
            acc_ref[...] += terms.reshape(acc_ref.shape)


def take_group(group, own_at, meta, x, s_own, carried):
    slots, bs = x.shape[0], x.shape[-1]
    first = carried is None
    n_own = 0 if s_own is None else s_own.shape[0]

    def x_index(c):
        def at(k, meta):
            return (jnp.maximum(meta[X_AT + (meta[GROUP_STEP_AT + group] * KB + k) * CB + c], 0), 0, 0)

        return at

    def s_index(r):
        def at(k, meta):
            slot = meta[GROUP_STEP_AT + group] // 2
            return (slot, jnp.maximum(meta[own_at + slot * RB * KB + r * KB + k], 0), 0, 0)

        return at

    acc_spec = pl.BlockSpec((RB, bs, CB * bs), lambda k, meta: (0, 0, 0))
    r_spec = pl.BlockSpec((1, 2, bs, CB * bs), lambda k, meta: (meta[GROUP_STEP_AT + group], 0, k, 0))
    in_specs = [pl.BlockSpec((1, bs, bs), x_index(c)) for c in range(CB)]
    operands = [x] * CB
    if n_own:
        in_specs += [pl.BlockSpec((1, 1, bs, bs), s_index(r)) for r in range(RB)]
        operands += [s_own] * RB
    aliases = {}
    if not first:
        aliases = {1 + len(operands): 0, 2 + len(operands): 1}
        in_specs += [acc_spec, pl.BlockSpec(memory_space=pl.ANY)]
        operands += list(carried)
    return pl.pallas_call(
        functools.partial(group_kernel, group, own_at, first, n_own),
        grid_spec=pltpu.PrefetchScalarGridSpec(
            num_scalar_prefetch=1, grid=(KB,), in_specs=in_specs, out_specs=[acc_spec, r_spec]
        ),
        out_shape=[
            jax.ShapeDtypeStruct((RB, bs, CB * bs), jnp.float32),
            jax.ShapeDtypeStruct((STEPS, 2, KB * bs, CB * bs), jnp.bfloat16),
        ],
        input_output_aliases=aliases,
        compiler_params=pltpu.CompilerParams(vmem_limit_bytes=32 * 2**20),
        cost_estimate=pl.CostEstimate(flops=3 * 2 * RB * KB * CB * bs**3, bytes_accessed=16 * 2**20, transcendentals=0),
        name="take_group",
    )(meta, *operands)


def finish_kernel(piece_at, step_at, n_out, meta, *refs):
    s_refs, (acc_in, r_ref, out_ref, acc_ref) = refs[:RB], refs[RB:]
    j, k = pl.program_id(0), pl.program_id(1)

    @pl.when((j == 0) & (k == 0))
    def _():
        acc_ref[...] = acc_in[...]

    blocks = []
    for r in range(RB):
        there = meta[piece_at + j * RB * KB + r * KB + k] >= 0
        blocks.append(jnp.where(there, s_refs[r][0, 0], 0.0))
    terms = product_terms(blocks, r_ref[0, 0], r_ref[0, 1])
    acc_ref[...] += terms.reshape(acc_ref.shape)
    bs = out_ref.shape[-1]

    @pl.when((j == pl.num_programs(0) - 1) & (k == pl.num_programs(1) - 1))
    def _():
        for m in range(n_out):
            row = meta[OUT_AT + 2 * m]
            col = pl.multiple_of(meta[OUT_AT + 2 * m + 1] * bs, bs)
            out_ref[m] = acc_ref[row, :, pl.ds(col, bs)]


def finish(piece_at, step_at, meta, pieces, acc, right, n_out):
    n_pieces, bs = pieces.shape[0], pieces.shape[-1]

    def s_index(r):
        def at(j, k, meta):
            return (j, jnp.maximum(meta[piece_at + j * RB * KB + r * KB + k], 0), 0, 0)

        return at

    return pl.pallas_call(
        functools.partial(finish_kernel, piece_at, step_at, n_out),
        grid_spec=pltpu.PrefetchScalarGridSpec(
            num_scalar_prefetch=1,
            grid=(n_pieces, KB),
            in_specs=[pl.BlockSpec((1, 1, bs, bs), s_index(r)) for r in range(RB)]
            + [
                pl.BlockSpec((RB, bs, CB * bs), lambda j, k, meta: (0, 0, 0)),
                pl.BlockSpec((1, 2, bs, CB * bs), lambda j, k, meta: (meta[step_at + j], 0, k, 0)),
            ],
            out_specs=pl.BlockSpec((n_out, bs, bs), lambda j, k, meta: (0, 0, 0)),
            scratch_shapes=[pltpu.VMEM((RB, bs, CB * bs), jnp.float32)],
        ),
        out_shape=jax.ShapeDtypeStruct((n_out, bs, bs), jnp.float32),
        compiler_params=pltpu.CompilerParams(vmem_limit_bytes=40 * 2**20),
        cost_estimate=pl.CostEstimate(
            flops=3 * 2 * n_pieces * RB * KB * CB * bs**3, bytes_accessed=18 * 2**20, transcendentals=0
        ),
        name="finish",
    )(meta, *([pieces] * RB), acc, right)


def per_device(s_blocks, s_list, x_blocks, x_list, c_list, owner):
    length, width = lax.axis_size("loop"), lax.axis_size("bcast")
    line, column = lax.axis_index("loop"), lax.axis_index("bcast")
    s_own, x_own, pairs, owner = s_blocks[0, 0], x_blocks[0, 0], c_list[0, 0], owner[0]
    depth, n_s, bs = s_own.shape[0], s_own.shape[1], s_own.shape[-1]
    n_x, n_out = x_own.shape[0], pairs.shape[0]

    swapped = width == 2
    if swapped:
        pieces = lax.ppermute(s_own, "bcast", [(0, 1), (1, 0)])
    else:
        held = lax.all_gather(s_own, "bcast")
        pieces = jnp.stack([held[owner[s], s // width] for s in range(STEPS)])

    near = [(g, (g - 1) % length if g % 2 == 0 else (g - 3) % length) for g in range(length)]
    far = [(g, (g - 3) % length if g % 2 == 0 else (g - 1) % length) for g in range(length)]
    groups = [x_own, lax.ppermute(x_own, "loop", near), lax.ppermute(x_own, "loop", far)]
    groups.append(lax.ppermute(groups[1], "loop", [(g, g ^ 1) for g in range(length)]))
    odd = line % 2
    group_step = jnp.stack([0 * odd, 3 - 2 * odd, 1 + 2 * odd, 0 * odd + 2])

    lists = jnp.concatenate([x_list.reshape(-1), s_list.reshape(-1)])
    lists = lax.all_gather(lists, ("loop", "bcast")).reshape(length, width, -1)
    mine = jnp.take(lists, (line + jnp.arange(STEPS)) % length, axis=0)
    x_places = jnp.take(mine, column, axis=1)[:, : 2 * n_x].reshape(STEPS, n_x, 2)
    s_places = mine[0, :, 2 * n_x :].reshape(width, depth, n_s, 2)
    steps = jnp.arange(STEPS)
    if swapped:
        own_flag = (owner == column).astype(jnp.int32)
        starts = width * jnp.arange(depth)
        piece_steps = starts + own_flag[::width]
        tables = [positions(s_places[column], RB, KB), positions(s_places[1 - column], RB, KB)]
    else:
        own_flag = jnp.zeros_like(steps)
        piece_steps = steps
        tables = [jnp.zeros((0,), jnp.int32), positions(s_places[owner, steps // width], RB, KB)]
    own_at = OUT_AT + 2 * n_out
    piece_at = own_at + tables[0].size
    step_at = piece_at + tables[1].size
    meta = jnp.concatenate(
        [
            part.reshape(-1).astype(jnp.int32)
            for part in (positions(x_places, KB, CB), own_flag, group_step, pairs, *tables, piece_steps)
        ]
    )

    carried = None
    for group in (0, 1, 3, 2):
        carried = take_group(group, own_at, meta, groups[group], s_own if swapped else None, carried)
    out = finish(piece_at, step_at, meta, pieces, *carried, n_out)
    return out[None, None]


def solution(mesh):
    return jax.shard_map(
        per_device,
        mesh=mesh,
        in_specs=(
            P("loop", "bcast", None, None, None, None),
            P("loop", "bcast", None, None, None),
            P("loop", "bcast", None, None, None),
            P("loop", "bcast", None, None),
            P("loop", "bcast", None, None),
            P("loop", None),
        ),
        out_specs=P("loop", "bcast", None, None, None),
        check_vma=False,
    )
```

```python
import functools

import jax
import jax.numpy as jnp
from jax import lax
from jax.experimental import pallas as pl
from jax.experimental.pallas import tpu as pltpu
from jax.sharding import PartitionSpec as P

RB = 3
KB = 4
CB = 4
STEPS = 4
UNROLL = 4
LIST_ROWS = 8


def pack_kernel(cuts, list_at, n_after, *refs):
    source, refs = refs[0], refs[1:]
    if list_at is not None:
        listed, refs = refs[0], refs[1:]
    target, sems = refs[n_after:]
    copies = [
        pltpu.make_async_copy(source.at[pl.ds(a, n)], target.at[pl.ds(b, n)], sems.at[i])
        for i, (a, b, n) in enumerate(cuts)
    ]
    if list_at is not None:
        copies.append(pltpu.make_async_copy(listed, target.at[pl.ds(list_at, LIST_ROWS)], sems.at[len(cuts)]))
    for copy in copies:
        copy.start()
    for copy in copies:
        copy.wait()


def pack(source, first, count, listed=None, after=()):
    columns = source.shape[1]
    part = count // 4
    cuts = [(first + i * part, i * part, part) for i in range(4)]
    rows = count + (0 if listed is None else LIST_ROWS)
    operands = [source] + ([] if listed is None else [listed]) + list(after)
    return pl.pallas_call(
        functools.partial(pack_kernel, cuts, None if listed is None else count, len(after)),
        in_specs=[pl.BlockSpec(memory_space=pl.ANY)] * len(operands),
        out_specs=pl.BlockSpec(memory_space=pl.ANY),
        out_shape=jax.ShapeDtypeStruct((rows, columns), source.dtype),
        scratch_shapes=[pltpu.SemaphoreType.DMA((5,))],
        cost_estimate=pl.CostEstimate(flops=0, bytes_accessed=8 * count * columns, transcendentals=0),
        name="pack",
    )(*operands)


def as_rows(places, columns):
    flat = places.reshape(-1).astype(jnp.float32)
    return jnp.pad(flat, (0, LIST_ROWS * columns - flat.size)).reshape(LIST_ROWS, columns)


def from_rows(packed, at, size):
    return packed[at : at + LIST_ROWS].reshape(-1)[:size].astype(jnp.int32)


def halves(values):
    high = values.astype(jnp.bfloat16)
    return high, (values - high.astype(jnp.float32)).astype(jnp.bfloat16)


def dot(left, right):
    return jnp.dot(left, right, preferred_element_type=jnp.float32)


def multiply_kernel(n_out, bs, plan, n_arrays, first, last, meta, *refs):
    arrays, refs = refs[:n_arrays], refs[n_arrays:]
    if not first:
        refs = refs[1:]
    if last:
        acc, out, r_map, o_map, todo, sems = refs
    else:
        acc, r_map, o_map, todo = refs
    if first:
        acc[...] = jnp.zeros_like(acc)
    for cell in range(RB * CB):
        o_map[cell] = -1
    for m in range(n_out):
        o_map[meta[2 * m] * CB + meta[2 * m + 1]] = m

    for left_at, first_block, n_left, list_at, uses in plan:
        left = arrays[left_at]
        for right_at, n_right, flag_at, right_list_at in uses:
            right = arrays[right_at]

            @pl.when(meta[flag_at] > 0)
            def _():
                for cell in range(KB * CB):
                    r_map[cell] = -1
                for j in range(n_right):
                    k, c = meta[right_list_at + 2 * j], meta[right_list_at + 2 * j + 1]
                    r_map[k * CB + c] = j

                def collect(i, count):
                    row, k = meta[list_at + 2 * i], meta[list_at + 2 * i + 1]
                    for c in range(CB):
                        j, m = r_map[k * CB + c], o_map[row * CB + c]
                        todo[count] = (i * 64 + jnp.maximum(j, 0)) * 64 + jnp.maximum(m, 0)
                        count = count + ((j >= 0) & (m >= 0)).astype(jnp.int32)
                    return count

                count = lax.fori_loop(0, n_left, collect, jnp.int32(0))
                for u in range(UNROLL):
                    todo[count + u] = n_out

                def several(q, carry):
                    for u in range(UNROLL):
                        code = todo[q * UNROLL + u]
                        i, j, m = code // 4096, (code // 64) % 64, code % 64
                        left_high, left_low = halves(left[pl.ds(pl.multiple_of((first_block + i) * bs, bs), bs), :])
                        right_high, right_low = halves(right[pl.ds(pl.multiple_of(j * bs, bs), bs), :])
                        acc[m] += (
                            dot(left_high, right_high) + dot(left_high, right_low) + dot(left_low, right_high)
                        )
                    return carry

                lax.fori_loop(0, (count + UNROLL - 1) // UNROLL, several, 0)

    if last:
        copies = [pltpu.make_async_copy(acc.at[m], out.at[m], sems.at[m]) for m in range(n_out)]
        for copy in copies:
            copy.start()
        for copy in copies:
            copy.wait()


def multiply(acc, pairs, parts, last=False, blocks=1):
    n_out = pairs.shape[0]
    arrays, scalars, plan = [], [pairs.reshape(-1)], []
    at = scalars[0].size

    def place(array):
        for index, other in enumerate(arrays):
            if other is array:
                return index
        arrays.append(array)
        return len(arrays) - 1

    def table(values):
        nonlocal at
        scalars.append(values.reshape(-1).astype(jnp.int32))
        at += values.size
        return at - values.size

    for left, first_block, left_list, uses in parts:
        entry = (place(left), first_block, left_list.size // 2, table(left_list))
        plan.append(entry + ([(place(r), r_list.size // 2, table(flag), table(r_list)) for r, r_list, flag in uses],))
    meta = jnp.concatenate(scalars)
    bs = arrays[0].shape[-1]
    first = acc is None
    vmem = pl.BlockSpec(memory_space=pltpu.VMEM)
    acc_shape = jax.ShapeDtypeStruct((n_out + 1, bs, bs), jnp.float32)
    most = max(n for _, _, n, _, _ in plan)
    scratch = [pltpu.SMEM(((KB + 1) * CB,), jnp.int32), pltpu.SMEM((RB * CB,), jnp.int32)]
    scratch.append(pltpu.SMEM((most * CB + UNROLL,), jnp.int32))
    if last:
        scratch.append(pltpu.SemaphoreType.DMA((n_out,)))
    out_shape, out_specs = [acc_shape], [vmem]
    if last:
        out_shape.append(jax.ShapeDtypeStruct((n_out, bs, bs), jnp.float32))
        out_specs.append(pl.BlockSpec(memory_space=pl.ANY))
    results = pl.pallas_call(
        functools.partial(multiply_kernel, n_out, bs, plan, len(arrays), first, last),
        in_specs=[pl.BlockSpec(memory_space=pltpu.SMEM)] + [vmem] * (len(arrays) + (not first)),
        out_specs=out_specs,
        out_shape=out_shape,
        scratch_shapes=scratch,
        input_output_aliases={} if first else {1 + len(arrays): 0},
        compiler_params=pltpu.CompilerParams(vmem_limit_bytes=32 * 2**20),
        cost_estimate=pl.CostEstimate(
            flops=blocks * 10 * 3 * 2 * bs**3, bytes_accessed=4 * 2**20, transcendentals=0
        ),
        name="multiply",
    )(meta, *arrays, *([] if first else [acc]))
    return results[-1]


def per_device(s_blocks, s_list, x_blocks, x_list, c_list, owner):
    length, width = lax.axis_size("loop"), lax.axis_size("bcast")
    line, column = lax.axis_index("loop"), lax.axis_index("bcast")
    pairs, owner = c_list[0, 0], owner[0]
    depth, n_s, bs = s_blocks.shape[2], s_blocks.shape[3], s_blocks.shape[-1]
    n_x = x_blocks.shape[2]
    x_rows = n_x * bs
    s_own = s_blocks.reshape(depth * n_s * bs, bs)
    s_own_list, x_own_list = s_list[0, 0], x_list[0, 0]
    swapped = width == 2

    cuts = [0, 3, n_s, depth * n_s - 3, depth * n_s]
    if swapped:
        partner = [(0, 1), (1, 0)]
        s_rows = as_rows(s_own_list, bs)
        sent = [pack(s_own, cuts[0] * bs, (cuts[1] - cuts[0]) * bs)]
        sent.append(pack(s_own, cuts[1] * bs, (cuts[2] - cuts[1]) * bs, s_rows, (sent[0],)))
        came = [lax.ppermute(chunk, "bcast", partner) for chunk in sent]
        for q in (2, 3):
            chunk = pack(s_own, cuts[q] * bs, (cuts[q + 1] - cuts[q]) * bs, None, (came[q - 2],))
            came.append(lax.ppermute(chunk, "bcast", partner))
        their_list = from_rows(came[1], (cuts[2] - cuts[1]) * bs, s_own_list.size).reshape(depth, n_s, 2)
        x_packed = pack(x_blocks.reshape(x_rows, bs), 0, x_rows, as_rows(x_own_list, bs), (sent[0],))
    else:
        held = lax.all_gather(s_own, "bcast")
        held_lists = lax.all_gather(s_own_list, "bcast")
        x_packed = pack(x_blocks.reshape(x_rows, bs), 0, x_rows, as_rows(x_own_list, bs))

    inside = [(g, g ^ 1) for g in range(length)]
    near = [(g, (g - 1) % length if g % 2 == 0 else (g - 3) % length) for g in range(length)]
    far = [(g, (g - 3) % length) for g in range(0, length, 2)]
    beside = lax.ppermute(x_packed, "loop", inside)
    close = lax.ppermute(x_packed, "loop", near)
    away = lax.ppermute(x_packed, "loop", far)
    handed = lax.ppermute(close, "loop", inside)
    odd = line % 2
    even = 1 - odd

    def group(packed):
        return packed, from_rows(packed, x_rows, x_own_list.size)

    own = (x_blocks.reshape(x_rows, bs), x_own_list)
    beside, close, away, handed = group(beside), group(close), group(away), group(handed)
    choices = [
        [(own, 1)],
        [(beside, even), (close, odd)],
        [(handed, 1)],
        [(close, even), (away, odd)],
    ]

    def uses(held_steps, late):
        found = []
        for step, held in held_steps:
            for (rows, places), applies in choices[step]:
                if late is None or (rows is away[0]) == late:
                    found.append((rows, places, jnp.asarray(held * applies, jnp.int32).reshape(1)))
        return found

    if not swapped:
        acc = None
        for step in range(STEPS):
            piece = lax.dynamic_index_in_dim(held, owner[step], 0, False)
            places = lax.dynamic_index_in_dim(held_lists, owner[step], 0, False)[step // width]
            part = (piece, step // width * n_s, places, uses([(step, 1)], None))
            acc = multiply(acc, pairs, [part], last=step == STEPS - 1, blocks=n_s)
        return acc[None, None]

    mine = (owner == column).astype(jnp.int32)
    own_parts, their_steps = [], []
    for slot in range(depth):
        steps = [2 * slot, 2 * slot + 1]
        own_parts.append((slot, [(s, mine[s]) for s in steps]))
        their_steps.append([(s, 1 - mine[s]) for s in steps])

    def chunk_part(q, late):
        slot = cuts[q] // n_s
        lo = cuts[q] - slot * n_s
        return (came[q], 0, their_list[slot, lo : lo + cuts[q + 1] - cuts[q]], uses(their_steps[slot], late))

    def own_part(slot, late):
        return (s_own, slot * n_s, s_own_list[slot], uses(own_parts[slot][1], late))

    acc = multiply(None, pairs, [own_part(0, False)], blocks=n_s)
    acc = multiply(acc, pairs, [chunk_part(0, False), chunk_part(1, False)], blocks=n_s)
    acc = multiply(acc, pairs, [own_part(1, False)], blocks=n_s)
    acc = multiply(acc, pairs, [chunk_part(2, False)], blocks=n_s)
    acc = multiply(acc, pairs, [own_part(1, True), chunk_part(2, True)], blocks=n_s)
    out = multiply(acc, pairs, [chunk_part(3, None)], last=True, blocks=3)
    return out[None, None]


def solution(mesh):
    return jax.shard_map(
        per_device,
        mesh=mesh,
        in_specs=(
            P("loop", "bcast", None, None, None, None),
            P("loop", "bcast", None, None, None),
            P("loop", "bcast", None, None, None),
            P("loop", "bcast", None, None),
            P("loop", "bcast", None, None),
            P("loop", None),
        ),
        out_specs=P("loop", "bcast", None, None, None),
        check_vma=False,
    )
```

```python
import functools

import jax
import jax.numpy as jnp
from jax import lax
from jax.experimental import pallas as pl
from jax.experimental.pallas import tpu as pltpu
from jax.sharding import PartitionSpec as P

RB = 3
KB = 4
CB = 4
STEPS = 4
UNROLL = 4
LIST_ROWS = 8
X_PARTS = 2
VMEM_LIMIT = 24 * 2**20
PACK_LIMIT = 56 * 2**20


def pack_kernel(cuts, *refs):
    target, sems = refs[-2:]
    copies = [
        pltpu.make_async_copy(refs[which].at[pl.ds(a, n)], target.at[pl.ds(b, n)], sems.at[i])
        for i, (which, a, b, n) in enumerate(cuts)
    ]
    for copy in copies:
        copy.start()
    for copy in copies:
        copy.wait()


def pack(source, first, count, listed=None, after=()):
    columns = source.shape[1]
    part = count // 4
    cuts = [(0, first + i * part, i * part, part) for i in range(4)]
    operands = [source]
    if listed is not None:
        cuts.append((1, 0, count, LIST_ROWS))
        operands.append(listed)
    operands += after
    rows = sum(n for _, _, _, n in cuts)
    return pl.pallas_call(
        functools.partial(pack_kernel, cuts),
        in_specs=[pl.BlockSpec(memory_space=pl.ANY)] * len(operands),
        out_specs=pl.BlockSpec(memory_space=pltpu.VMEM),
        out_shape=jax.ShapeDtypeStruct((rows, columns), source.dtype),
        scratch_shapes=[pltpu.SemaphoreType.DMA((len(cuts),))],
        compiler_params=pltpu.CompilerParams(vmem_limit_bytes=PACK_LIMIT),
        cost_estimate=pl.CostEstimate(flops=0, bytes_accessed=8 * count * columns, transcendentals=0),
        name="pack",
    )(*operands)


def as_rows(places, columns):
    flat = places.reshape(-1).astype(jnp.float32)
    return jnp.pad(flat, (0, LIST_ROWS * columns - flat.size)).reshape(LIST_ROWS, columns)


def from_rows(packed, at, size):
    return packed[at : at + LIST_ROWS].reshape(-1)[:size].astype(jnp.int32)


def halves(values):
    high = values.astype(jnp.bfloat16)
    return high, (values - high.astype(jnp.float32)).astype(jnp.bfloat16)


def dot(left, right):
    return jnp.dot(left, right, preferred_element_type=jnp.float32)


def multiply_kernel(n_out, bs, plan, n_tables, n_arrays, first, last, *refs):
    tables, refs = refs[:n_tables], refs[n_tables:]
    meta = tables[0]
    arrays, refs = refs[:n_arrays], refs[n_arrays:]
    if not first:
        refs = refs[1:]
    if last:
        acc, out, r_map, o_map, todo, sems = refs
    else:
        acc, r_map, o_map, todo = refs
    if first:
        acc[...] = jnp.zeros_like(acc)
    for cell in range(RB * CB):
        o_map[cell] = -1
    for m in range(n_out):
        o_map[meta[2 * m] * CB + meta[2 * m + 1]] = m

    for left_at, first_block, n_left, table_at, list_at, uses in plan:
        entries = tables[table_at]
        left = arrays[left_at]
        for right_at, n_right, flag_at, right_list_at in uses:
            right = arrays[right_at]

            @pl.when(meta[flag_at] > 0)
            def _():
                for cell in range(KB * CB):
                    r_map[cell] = -1
                for j in range(n_right):
                    k, c = meta[right_list_at + 2 * j], meta[right_list_at + 2 * j + 1]
                    r_map[k * CB + c] = j

                def collect(i, count):
                    row, k = entries[list_at + 2 * i], entries[list_at + 2 * i + 1]
                    for c in range(CB):
                        j, m = r_map[k * CB + c], o_map[row * CB + c]
                        todo[count] = (i * 64 + jnp.maximum(j, 0)) * 64 + jnp.maximum(m, 0)
                        count = count + ((j >= 0) & (m >= 0)).astype(jnp.int32)
                    return count

                count = lax.fori_loop(0, n_left, collect, jnp.int32(0))
                for u in range(UNROLL):
                    todo[count + u] = n_out

                def several(q, carry):
                    for u in range(UNROLL):
                        code = todo[q * UNROLL + u]
                        i, j, m = code // 4096, (code // 64) % 64, code % 64
                        left_high, left_low = halves(left[pl.ds(pl.multiple_of((first_block + i) * bs, bs), bs), :])
                        right_high, right_low = halves(right[pl.ds(pl.multiple_of(j * bs, bs), bs), :])
                        acc[m] += (
                            dot(left_high, right_high) + dot(left_high, right_low) + dot(left_low, right_high)
                        )
                    return carry

                lax.fori_loop(0, (count + UNROLL - 1) // UNROLL, several, 0)

    if last:
        copies = [pltpu.make_async_copy(acc.at[m], out.at[m], sems.at[m]) for m in range(n_out)]
        for copy in copies:
            copy.start()
        for copy in copies:
            copy.wait()


def multiply(acc, pairs, parts, last=False, late_list=None):
    n_out = pairs.shape[0]
    arrays, scalars, plan = [], [pairs.reshape(-1)], []
    at = scalars[0].size

    def place(array):
        for index, other in enumerate(arrays):
            if other is array:
                return index
        arrays.append(array)
        return len(arrays) - 1

    def table(values):
        nonlocal at
        scalars.append(values.reshape(-1).astype(jnp.int32))
        at += values.size
        return at - values.size

    for left, first_block, left_list, uses in parts:
        if isinstance(left_list, tuple):
            entry = (place(left), first_block, left_list[1], 1, left_list[0])
        else:
            entry = (place(left), first_block, left_list.size // 2, 0, table(left_list))
        plan.append(entry + ([(place(r), r_list.size // 2, table(flag), table(r_list)) for r, r_list, flag in uses],))
    tables = [jnp.concatenate(scalars)] + ([] if late_list is None else [late_list])
    bs = arrays[0].shape[-1]
    first = acc is None
    vmem = pl.BlockSpec(memory_space=pltpu.VMEM)
    acc_shape = jax.ShapeDtypeStruct((n_out + 1, bs, bs), jnp.float32)
    most = max(n for _, _, n, _, _, _ in plan)
    scratch = [pltpu.SMEM(((KB + 1) * CB,), jnp.int32), pltpu.SMEM((RB * CB,), jnp.int32)]
    scratch.append(pltpu.SMEM((most * CB + UNROLL,), jnp.int32))
    if last:
        scratch.append(pltpu.SemaphoreType.DMA((n_out,)))
    out_shape, out_specs = [acc_shape], [vmem]
    if last:
        out_shape.append(jax.ShapeDtypeStruct((n_out, bs, bs), jnp.float32))
        out_specs.append(pl.BlockSpec(memory_space=pl.ANY))
    results = pl.pallas_call(
        functools.partial(multiply_kernel, n_out, bs, plan, len(tables), len(arrays), first, last),
        in_specs=[pl.BlockSpec(memory_space=pltpu.SMEM)] * len(tables) + [vmem] * (len(arrays) + (not first)),
        out_specs=out_specs,
        out_shape=out_shape,
        scratch_shapes=scratch,
        input_output_aliases={} if first else {len(tables) + len(arrays): 0},
        compiler_params=pltpu.CompilerParams(vmem_limit_bytes=VMEM_LIMIT),
        cost_estimate=pl.CostEstimate(
            flops=5 * 10**9, bytes_accessed=4 * 2**20, transcendentals=0
        ),
        name="multiply",
    )(*tables, *arrays, *([] if first else [acc]))
    return results[-1]


def per_device(s_blocks, s_list, x_blocks, x_list, c_list, owner):
    length, width = lax.axis_size("loop"), lax.axis_size("bcast")
    line, column = lax.axis_index("loop"), lax.axis_index("bcast")
    pairs, owner = c_list[0, 0], owner[0]
    depth, n_s, bs = s_blocks.shape[2], s_blocks.shape[3], s_blocks.shape[-1]
    n_x = x_blocks.shape[2]
    s_own = s_blocks.reshape(depth * n_s * bs, bs)
    s_own_list, x_own_list = s_list[0, 0], x_list[0, 0]
    swapped = width == 2

    if swapped:
        partner = [(0, 1), (1, 0)]
        came = lax.ppermute(s_own, "bcast", partner)
        their_list = lax.ppermute(s_own_list.reshape(-1), "bcast", partner)
    else:
        held = lax.all_gather(s_own, "bcast")
        held_lists = lax.all_gather(s_own_list, "bcast")

    inside = [(g, g ^ 1) for g in range(length)]
    near = [(g, (g - 1) % length if g % 2 == 0 else (g - 3) % length) for g in range(length)]
    far = [(g, (g - 3) % length if g % 2 == 0 else (g - 1) % length) for g in range(length)]
    x_own = x_blocks.reshape(n_x * bs, bs)
    share = n_x // X_PARTS
    x_parts = []
    for p in range(X_PARTS):
        rows = as_rows(x_own_list[p * share : (p + 1) * share], bs)
        x_parts.append(jnp.concatenate([x_own[p * share * bs : (p + 1) * share * bs], rows]))

    def moved(parts, pairs):
        return [lax.ppermute(part, "loop", pairs) for part in parts]

    def listed(parts):
        return [(part, from_rows(part, share * bs, 2 * share)) for part in parts]

    close_parts = moved(x_parts, near)
    groups = {
        "own": [(x_own, x_own_list)],
        "close": listed(close_parts),
        "handed": listed(moved(close_parts, inside)),
    }
    odd = line % 2
    even = 1 - odd
    choices = [
        [("own", 1)],
        [("away", even), ("close", odd)],
        [("handed", 1)],
        [("close", even), ("away", odd)],
    ]

    def uses(held_steps, names):
        found = []
        for step, held in held_steps:
            for name, applies in choices[step]:
                if name in names:
                    flag = jnp.asarray(held * applies, jnp.int32).reshape(1)
                    found += [(rows, places, flag) for rows, places in groups[name]]
        return found

    if not swapped:
        groups["away"] = listed(moved(x_parts, far))
        acc = None
        for step in range(STEPS):
            piece = lax.dynamic_index_in_dim(held, owner[step], 0, False)
            places = lax.dynamic_index_in_dim(held_lists, owner[step], 0, False)[step // width]
            part = (piece, step // width * n_s, places, uses([(step, 1)], groups))
            acc = multiply(acc, pairs, [part], last=step == STEPS - 1)
        return acc[None, None]

    mine = (owner == column).astype(jnp.int32)

    def own_part(slot, *names):
        steps = [(s, mine[s]) for s in (2 * slot, 2 * slot + 1)]
        return (s_own, slot * n_s, s_own_list[slot], uses(steps, names))

    def their_part(slot, *names):
        steps = [(s, 1 - mine[s]) for s in (2 * slot, 2 * slot + 1)]
        return (came, slot * n_s, (slot * 2 * n_s, n_s), uses(steps, names))

    packed = pack(x_own, 0, n_x * bs, as_rows(x_own_list, bs), (close_parts[0],))
    packed = lax.ppermute(packed, "loop", far)
    groups["away"] = [(packed, from_rows(packed, n_x * bs, x_own_list.size))]
    acc = multiply(None, pairs, [own_part(0, "own", "close"), own_part(1, "close", "handed")])
    acc = multiply(acc, pairs, [own_part(0, "away"), own_part(1, "away")])
    their_parts = [their_part(0, "own", "close", "away"), their_part(1, "close", "handed", "away")]
    out = multiply(acc, pairs, their_parts, last=True, late_list=their_list)
    return out[None, None]


def solution(mesh):
    return jax.shard_map(
        per_device,
        mesh=mesh,
        in_specs=(
            P("loop", "bcast", None, None, None, None),
            P("loop", "bcast", None, None, None),
            P("loop", "bcast", None, None, None),
            P("loop", "bcast", None, None),
            P("loop", "bcast", None, None),
            P("loop", None),
        ),
        out_specs=P("loop", "bcast", None, None, None),
        check_vma=False,
    )
```

```python
import functools

import jax
import jax.numpy as jnp
from jax import lax
from jax.experimental import pallas as pl
from jax.experimental.pallas import tpu as pltpu
from jax.sharding import PartitionSpec as P

RB = 3
KB = 4
CB = 4
STEPS = 4
UNROLL = 4
LIST_ROWS = 8
X_PARTS = 3
VMEM = pl.BlockSpec(memory_space=pltpu.VMEM)
SMEM = pl.BlockSpec(memory_space=pltpu.SMEM)


def pack_kernel(share, places, x, *refs):
    *targets, sems = refs
    n_x, bs = places.shape[0], x.shape[-1]
    cuts = [(0, n_x)] + [(p * share, share) for p in range(n_x // share)]
    copies = [
        pltpu.make_async_copy(x.at[pl.ds(first * bs, n * bs)], target.at[pl.ds(0, n * bs)], sems.at[i])
        for i, (target, (first, n)) in enumerate(zip(targets, cuts))
    ]
    for copy in copies:
        copy.start()
    lane = lax.broadcasted_iota(jnp.int32, (LIST_ROWS, bs), 1)
    for target, (first, n) in zip(targets, cuts):
        rows = jnp.zeros((LIST_ROWS, bs), jnp.float32)
        for j in range(n):
            for d in range(2):
                rows = jnp.where(lane == 2 * j + d, places[first + j, d].astype(jnp.float32), rows)
        target[n * bs : n * bs + LIST_ROWS] = rows
    for copy in copies:
        copy.wait()


def pack(x, places, share):
    n_x, bs = places.shape[0], x.shape[-1]
    sizes = [n_x] + [share] * (n_x // share)
    return pl.pallas_call(
        functools.partial(pack_kernel, share),
        in_specs=[SMEM, pl.BlockSpec(memory_space=pl.ANY)],
        out_specs=[VMEM] * len(sizes),
        out_shape=[jax.ShapeDtypeStruct((n * bs + LIST_ROWS, bs), x.dtype) for n in sizes],
        scratch_shapes=[pltpu.SemaphoreType.DMA((len(sizes),))],
        compiler_params=pltpu.CompilerParams(vmem_limit_bytes=16 * 2**20),
        cost_estimate=pl.CostEstimate(flops=0, bytes_accessed=2**20, transcendentals=0),
        name="pack",
    )(places, x)


def halves(values):
    high = values.astype(jnp.bfloat16)
    return high, (values - high.astype(jnp.float32)).astype(jnp.bfloat16)


def dot(left, right):
    return jnp.dot(left, right, preferred_element_type=jnp.float32)


def block(rows, index, bs):
    return rows[pl.ds(pl.multiple_of(index * bs, bs), bs), :]


def fill_map(target, size, read, count, columns):
    for cell in range(size):
        target[cell] = -1
    for entry in range(count):
        target[read(entry, 0) * columns + read(entry, 1)] = entry


def add_products(acc, n_out, bs, maps, todo, left_place, n_left, left, first, right):
    r_map, o_map = maps

    def collect(i, count):
        row, k = left_place(i)
        for c in range(CB):
            j, m = r_map[k * CB + c], o_map[row * CB + c]
            todo[count] = (i * 64 + jnp.maximum(j, 0)) * 64 + jnp.maximum(m, 0)
            count = count + ((j >= 0) & (m >= 0)).astype(jnp.int32)
        return count

    count = lax.fori_loop(0, n_left, collect, jnp.int32(0))
    for u in range(UNROLL):
        todo[count + u] = n_out

    def several(q, carry):
        for u in range(UNROLL):
            code = todo[q * UNROLL + u]
            i, j, m = code // 4096, (code // 64) % 64, code % 64
            left_high, left_low = halves(block(left, first + i, bs))
            right_high, right_low = right(j)
            acc[m] += dot(left_high, right_high) + dot(left_high, right_low) + dot(left_low, right_high)
        return carry

    lax.fori_loop(0, (count + UNROLL - 1) // UNROLL, several, 0)


def own_kernel(slot, n_left, n_x, plan, n_arrays, chooses, owner, pairs, left_list, left, *refs):
    arrays, refs = refs[:n_arrays], refs[n_arrays:]
    before, refs = (refs[0], refs[1:]) if slot and chooses else (None, refs)
    acc, refs = refs[0], refs[1:]
    if chooses:
        chosen, chosen_list, refs = refs[0], refs[1], refs[2:]
    here_lists, there_lists, refs = refs[:X_PARTS], refs[X_PARTS : 2 * X_PARTS], refs[2 * X_PARTS :]
    left_rows, here_rows, there_rows, r_map, o_map, todo, sems = refs
    n_out, bs = pairs.shape[0], left.shape[-1]
    place, column = lax.axis_index("loop") % 4, lax.axis_index("bcast")

    own_copies = [pltpu.make_async_copy(left.at[pl.ds(slot * n_left * bs, n_left * bs)], left_rows, sems.at[0])]
    if before is not None:
        own_copies.append(pltpu.make_async_copy(before, acc, sems.at[1]))
    for copy in own_copies:
        copy.start()

    def fetch(at, parts, rows, lists):
        copies = []
        for p, array in enumerate(parts):
            n = n_x // len(parts)
            right = arrays[array]
            target = rows.at[pl.ds(p * n * bs, n * bs)]
            copies.append(pltpu.make_async_copy(right.at[pl.ds(0, n * bs)], target, sems.at[at + 2 * p]))
            listed = right.at[pl.ds(n * bs, LIST_ROWS)]
            copies.append(pltpu.make_async_copy(listed, lists[p], sems.at[at + 2 * p + 1]))
        return copies

    def place_in(lists, count):
        n = n_x // count
        return lambda j, d: lists[j // n][0, 2 * (j % n) + d].astype(jnp.int32)

    def each(then):
        for step, places, parts in plan:
            applies = functools.reduce(jnp.logical_or, [place == value for value in places])
            mine = owner[step] == column if chooses else True
            pl.when(applies & mine)(functools.partial(then, parts, True))
            if chooses:
                pl.when(applies & jnp.logical_not(mine))(functools.partial(then, parts, False))

    def start(parts, here):
        for copy in fetch(2, parts, here_rows, here_lists) if here else fetch(
            2 + 2 * X_PARTS, parts, there_rows, there_lists
        ):
            copy.start()

    def land(wanted, parts, here):
        if here != wanted:
            return
        if here:
            for copy in fetch(2, parts, here_rows, here_lists):
                copy.wait()
            fill_map(r_map, KB * CB, place_in(here_lists, len(parts)), n_x, CB)
            return
        for copy in fetch(2 + 2 * X_PARTS, parts, there_rows, there_lists):
            copy.wait()
        read = place_in(there_lists, len(parts))
        for j in range(n_x):
            for d in range(2):
                chosen_list[2 * j + d] = read(j, d)

    def left_place(i):
        return left_list[slot * n_left + i, 0], left_list[slot * n_left + i, 1]

    each(start)
    fill_map(o_map, RB * CB, lambda m, d: pairs[m, d], n_out, CB)
    if before is None:
        acc[...] = jnp.zeros_like(acc)
    each(functools.partial(land, True))
    for copy in own_copies:
        copy.wait()
    add_products(
        acc, n_out, bs, (r_map, o_map), todo, left_place, n_left, left_rows, 0, lambda j: halves(block(here_rows, j, bs))
    )
    if chooses:
        each(functools.partial(land, False))

        def split(j, carry):
            chosen[j, 0], chosen[j, 1] = halves(block(there_rows, j, bs))
            return carry

        lax.fori_loop(0, n_x, split, 0)


def own_products(owner, pairs, left, slot, left_list, n_left, choices, before, chooses):
    bs, n_out = left.shape[-1], pairs.shape[0]
    arrays, plan = [], []
    for step, places, parts in choices:
        at = []
        for part in parts:
            known = [i for i, other in enumerate(arrays) if other is part]
            if not known:
                known = [len(arrays)]
                arrays.append(part)
            at.append(known[0])
        plan.append((step, places, at))
    n_x = sum(part.shape[0] // bs for part in choices[0][2])
    anywhere = pl.BlockSpec(memory_space=pl.ANY)
    operands = [left, *arrays] + ([before] if slot and chooses else [])
    out_shape, out_specs = [jax.ShapeDtypeStruct((n_out + 1, bs, bs), jnp.float32)], [VMEM]
    if chooses:
        out_shape.append(jax.ShapeDtypeStruct((n_x, 2, bs, bs), jnp.bfloat16))
        out_shape.append(jax.ShapeDtypeStruct((2 * n_x,), jnp.int32))
        out_specs += [VMEM, SMEM]
    return pl.pallas_call(
        functools.partial(own_kernel, slot, n_left, n_x, plan, len(arrays), chooses),
        in_specs=[SMEM] * 3 + [anywhere] * len(operands),
        out_specs=out_specs,
        out_shape=out_shape,
        scratch_shapes=[pltpu.SMEM((LIST_ROWS, bs), jnp.float32)] * (2 * X_PARTS)
        + [
            pltpu.VMEM((n_left * bs, bs), jnp.float32),
            pltpu.VMEM((n_x * bs, bs), jnp.float32),
            pltpu.VMEM((n_x * bs, bs), jnp.float32),
            pltpu.SMEM(((KB + 1) * CB,), jnp.int32),
            pltpu.SMEM((RB * CB,), jnp.int32),
            pltpu.SMEM((n_left * CB + UNROLL,), jnp.int32),
            pltpu.SemaphoreType.DMA((2 + 4 * X_PARTS,)),
        ],
        compiler_params=pltpu.CompilerParams(vmem_limit_bytes=OWN_LIMIT),
        cost_estimate=pl.CostEstimate(flops=0, bytes_accessed=2**20, transcendentals=0),
        name="own_products",
    )(owner, pairs, left_list, *operands)


OWN_LIMIT = 32 * 2**20
LAST_LIMIT = 24 * 2**20


def last_kernel(depth, n_left, n_x, pairs, late, *refs):
    right_lists, refs = refs[:depth], refs[depth:]
    left, before, chosen, refs = refs[0], refs[1], refs[2 : depth + 2], refs[depth + 2 :]
    out, acc, left_rows, r_map, o_map, todo, sems = refs
    n_out, bs = pairs.shape[0], left.shape[-1]
    size = n_left * bs
    fetched = [
        pltpu.make_async_copy(left.at[pl.ds(slot * size, size)], left_rows.at[pl.ds(slot * size, size)], sems.at[slot])
        for slot in range(depth)
    ]
    for copy in fetched:
        copy.start()
    for m in range(n_out):
        acc[m] = before[m]
    fill_map(o_map, RB * CB, lambda m, d: pairs[m, d], n_out, CB)
    for slot in range(depth):
        fill_map(r_map, KB * CB, lambda j, d: right_lists[slot][2 * j + d], n_x, CB)
        fetched[slot].wait()
        add_products(
            acc, n_out, bs, (r_map, o_map), todo,
            lambda i: (late[2 * (slot * n_left + i)], late[2 * (slot * n_left + i) + 1]),
            n_left, left_rows, slot * n_left,
            lambda j: (chosen[slot][j, 0], chosen[slot][j, 1]),
        )
    copies = [pltpu.make_async_copy(acc.at[m], out.at[m], sems.at[depth + m]) for m in range(n_out)]
    for copy in copies:
        copy.start()
    for copy in copies:
        copy.wait()


def last_products(pairs, late, right_lists, left, n_left, before, chosen):
    bs = left.shape[-1]
    n_out, n_x, depth = pairs.shape[0], chosen[0].shape[0], len(chosen)
    anywhere = pl.BlockSpec(memory_space=pl.ANY)
    return pl.pallas_call(
        functools.partial(last_kernel, depth, n_left, n_x),
        in_specs=[SMEM] * (2 + depth) + [anywhere] + [VMEM] * (1 + depth),
        out_specs=anywhere,
        out_shape=jax.ShapeDtypeStruct((n_out, bs, bs), jnp.float32),
        scratch_shapes=[
            pltpu.VMEM((n_out + 1, bs, bs), jnp.float32),
            pltpu.VMEM((depth * n_left * bs, bs), jnp.float32),
            pltpu.SMEM(((KB + 1) * CB,), jnp.int32),
            pltpu.SMEM((RB * CB,), jnp.int32),
            pltpu.SMEM((n_left * CB + UNROLL,), jnp.int32),
            pltpu.SemaphoreType.DMA((depth + n_out,)),
        ],
        compiler_params=pltpu.CompilerParams(vmem_limit_bytes=LAST_LIMIT),
        cost_estimate=pl.CostEstimate(flops=0, bytes_accessed=2**20, transcendentals=0),
        name="last_products",
    )(pairs, late, *right_lists, left, before, *chosen)


def per_device(s_blocks, s_list, x_blocks, x_list, c_list, owner):
    length, width = lax.axis_size("loop"), lax.axis_size("bcast")
    pairs, owner = c_list[0, 0], owner[0]
    depth, n_s, bs = s_blocks.shape[2], s_blocks.shape[3], s_blocks.shape[-1]
    n_x = x_blocks.shape[2]
    s_own, x_own = s_blocks.reshape(depth * n_s * bs, bs), x_blocks.reshape(n_x * bs, bs)
    s_own_list, x_own_list = s_list.reshape(depth * n_s, 2), x_list[0, 0]

    swapped = width == 2
    if swapped:
        partner = [(0, 1), (1, 0)]
        came = lax.ppermute(s_own, "bcast", partner)
        their_list = lax.ppermute(s_own_list.reshape(-1), "bcast", partner)
    else:
        held = lax.all_gather(s_own, "bcast")
        held_lists = lax.all_gather(s_own_list, "bcast")

    share = n_x // X_PARTS
    everything, *parts = pack(x_own, x_own_list, share)

    def moved(packed, to):
        return [lax.ppermute(part, "loop", [(g, (g + to[g % 4]) % length) for g in range(length)]) for part in packed]

    first = moved(parts, (-1, 1, -1, -3))
    second = moved(first, (1, -1, -3, -1))
    third = [lax.ppermute(part, "loop", [(g, g - 1) for g in range(3, length, 4)]) for part in second]
    other = moved([everything], (-3, -1, -3, -1))

    choices = [
        (0, (0, 1, 2, 3), [everything]),
        (1, (1, 3), first),
        (1, (0, 2), other),
        (2, (0, 1, 2, 3), second),
        (3, (0,), first),
        (3, (2,), third),
        (3, (1, 3), other),
    ]

    if not swapped:
        total = 0
        for step in range(STEPS):
            piece = lax.dynamic_index_in_dim(held, owner[step], 0, False)
            places = lax.dynamic_index_in_dim(held_lists, owner[step], 0, False)
            fit = [choice for choice in choices if choice[0] == step]
            total = total + own_products(owner, pairs, piece, step // width, places, n_s, fit, None, False)[0]
        return total[None, None, : pairs.shape[0]]

    acc, chosen, right_lists = None, [], []
    for slot in range(depth):
        fit = [choice for choice in choices if choice[0] // width == slot]
        acc, split, places = own_products(owner, pairs, s_own, slot, s_own_list, n_s, fit, acc, True)
        chosen.append(split)
        right_lists.append(places)
    return last_products(pairs, their_list, right_lists, came, n_s, acc, chosen)[None, None]


def solution(mesh):
    return jax.shard_map(
        per_device,
        mesh=mesh,
        in_specs=(
            P("loop", "bcast", None, None, None, None),
            P("loop", "bcast", None, None, None),
            P("loop", "bcast", None, None, None),
            P("loop", "bcast", None, None),
            P("loop", "bcast", None, None),
            P("loop", None),
        ),
        out_specs=P("loop", "bcast", None, None, None),
        check_vma=False,
    )
```

```python
import functools

import jax
import jax.numpy as jnp
from jax import lax
from jax.experimental import pallas as pl
from jax.experimental.pallas import tpu as pltpu
from jax.sharding import PartitionSpec as P

RB = 3
KB = 4
CB = 4
STEPS = 4
LIST_ROWS = 8
X_PARTS = 3
LAST = 0
VMEM = pl.BlockSpec(memory_space=pltpu.VMEM)
SMEM = pl.BlockSpec(memory_space=pltpu.SMEM)


def pack_kernel(share, places, x, *refs):
    *targets, sems = refs
    n_x, bs = places.shape[0], x.shape[-1]
    cuts = [(0, n_x)] + [(p * share, share) for p in range(n_x // share)]
    copies = [
        pltpu.make_async_copy(x.at[pl.ds(first * bs, n * bs)], target.at[pl.ds(0, n * bs)], sems.at[i])
        for i, (target, (first, n)) in enumerate(zip(targets, cuts))
    ]
    for copy in copies:
        copy.start()
    lane = lax.broadcasted_iota(jnp.int32, (LIST_ROWS, bs), 1)
    for target, (first, n) in zip(targets, cuts):
        rows = jnp.zeros((LIST_ROWS, bs), jnp.float32)
        for j in range(n):
            for d in range(2):
                rows = jnp.where(lane == 2 * j + d, places[first + j, d].astype(jnp.float32), rows)
        target[n * bs : n * bs + LIST_ROWS] = rows
    for copy in copies:
        copy.wait()


def pack(x, places, share):
    n_x, bs = places.shape[0], x.shape[-1]
    sizes = [n_x] + [share] * (n_x // share)
    return pl.pallas_call(
        functools.partial(pack_kernel, share),
        in_specs=[SMEM, pl.BlockSpec(memory_space=pl.ANY)],
        out_specs=[VMEM] * len(sizes),
        out_shape=[jax.ShapeDtypeStruct((n * bs + LIST_ROWS, bs), x.dtype) for n in sizes],
        scratch_shapes=[pltpu.SemaphoreType.DMA((len(sizes),))],
        compiler_params=pltpu.CompilerParams(vmem_limit_bytes=16 * 2**20),
        cost_estimate=pl.CostEstimate(flops=0, bytes_accessed=2**20, transcendentals=0),
        name="pack",
    )(places, x)


def halves(values):
    high = values.astype(jnp.bfloat16)
    return high, (values - high.astype(jnp.float32)).astype(jnp.bfloat16)


def dot(left, right):
    return jnp.dot(left, right, preferred_element_type=jnp.float32)


def block(rows, index, bs):
    return rows[pl.ds(pl.multiple_of(index * bs, bs), bs), :]


def fill_map(target, size, read, count, columns):
    for cell in range(size):
        target[cell] = -1
    for entry in range(count):
        target[read(entry, 0) * columns + read(entry, 1)] = entry


def add_products(acc, n_out, bs, maps, todo, left_place, n_left, left, right):
    r_map, o_map = maps
    unroll = todo.shape[0] - n_left * CB

    def collect(i, count):
        row, base = left_place(i)
        for c in range(CB):
            j, m = r_map[base + c], o_map[row * CB + c]
            todo[count] = (i * 64 + jnp.maximum(j, 0)) * 64 + jnp.maximum(m, 0)
            count = count + ((j >= 0) & (m >= 0)).astype(jnp.int32)
        return count

    count = lax.fori_loop(0, n_left, collect, jnp.int32(0))
    for u in range(unroll):
        todo[count + u] = n_out

    def several(q, carry):
        for u in range(unroll):
            code = todo[q * unroll + u]
            i, j, m = code // 4096, (code // 64) % 64, code % 64
            left_high, left_low = halves(block(left, i, bs))
            right_high, right_low = right(j)
            acc[m] += dot(left_high, right_high) + dot(left_high, right_low) + dot(left_low, right_high)
        return carry

    lax.fori_loop(0, (count + unroll - 1) // unroll, several, 0)


def own_kernel(slot, n_left, n_x, plan, n_arrays, chooses, last, owner, pairs, left_list, *refs):
    refs = list(refs)

    def take(count):
        taken, refs[:count] = refs[:count], []
        return taken

    adds = chooses and slot > 0
    (list_before,) = take(1) if adds else (None,)
    (left,), arrays = take(1), take(n_arrays)
    acc_before, chosen_before = take(2) if adds else (None, None)
    (acc_out,) = take(1)
    chosen_out, chosen_list = take(2) if chooses else (None, None)
    here_lists, there_lists = take(X_PARTS), take(X_PARTS)
    left_rows, here_rows, there_rows, r_map, o_map, todo, sems = take(7)
    acc, chosen = (acc_out, chosen_out) if last else take(2)
    n_out, bs = pairs.shape[0], left.shape[-1]
    place, column = lax.axis_index("loop") % 4, lax.axis_index("bcast")
    mark = slot * n_x if last and chooses else 0

    own_copies = [pltpu.make_async_copy(left.at[pl.ds(slot * n_left * bs, n_left * bs)], left_rows, sems.at[0])]
    if adds:
        own_copies.append(pltpu.make_async_copy(acc_before, acc, sems.at[1]))
        own_copies.append(pltpu.make_async_copy(chosen_before, chosen.at[pl.ds(0, mark)], sems.at[2]))
    for copy in own_copies:
        copy.start()

    def fetch(at, parts, rows, lists):
        copies = []
        for p, array in enumerate(parts):
            n = n_x // len(parts)
            right = arrays[array]
            target = rows.at[pl.ds(p * n * bs, n * bs)]
            copies.append(pltpu.make_async_copy(right.at[pl.ds(0, n * bs)], target, sems.at[at + 2 * p]))
            listed = right.at[pl.ds(n * bs, LIST_ROWS)]
            copies.append(pltpu.make_async_copy(listed, lists[p], sems.at[at + 2 * p + 1]))
        return copies

    def copies_of(parts, here):
        if here:
            return fetch(5, parts, here_rows, here_lists)
        return fetch(5 + 2 * X_PARTS, parts, there_rows, there_lists)

    def place_in(lists, count):
        n = n_x // count
        return lambda j, d: lists[j // n][0, 2 * (j % n) + d].astype(jnp.int32)

    def each(then):
        for step, places, parts in plan:
            applies = functools.reduce(jnp.logical_or, [place == value for value in places])
            mine = owner[step] == column if chooses else True
            pl.when(applies & mine)(functools.partial(then, parts, True))
            if chooses:
                pl.when(applies & jnp.logical_not(mine))(functools.partial(then, parts, False))

    def start(parts, here):
        for copy in copies_of(parts, here):
            copy.start()

    def land(wanted, parts, here):
        if here != wanted:
            return
        for copy in copies_of(parts, here):
            copy.wait()
        if here:
            fill_map(r_map, KB * CB, place_in(here_lists, len(parts)), n_x, CB)
            return
        read = place_in(there_lists, len(parts))
        for j in range(n_x):
            for d in range(2):
                chosen_list[2 * (slot * n_x + j) + d] = read(j, d)

    def left_place(i):
        return left_list[slot * n_left + i, 0], left_list[slot * n_left + i, 1] * CB

    each(start)
    fill_map(o_map, RB * CB, lambda m, d: pairs[m, d], n_out, CB)
    if adds:
        for q in range(2 * slot * n_x):
            chosen_list[q] = list_before[q]
    else:
        acc[...] = jnp.zeros_like(acc)
    each(functools.partial(land, True))
    for copy in own_copies:
        copy.wait()
    add_products(
        acc, n_out, bs, (r_map, o_map), todo, left_place, n_left, left_rows, lambda j: halves(block(here_rows, j, bs))
    )
    if not chooses:
        return
    out_copies = []
    if not last:
        out_copies.append(pltpu.make_async_copy(acc, acc_out, sems.at[3]))
        out_copies[0].start()
    each(functools.partial(land, False))

    def split(j, carry):
        chosen[mark + j, 0], chosen[mark + j, 1] = halves(block(there_rows, j, bs))
        return carry

    lax.fori_loop(0, n_x, split, 0)
    if not last:
        out_copies.append(pltpu.make_async_copy(chosen, chosen_out, sems.at[4]))
        out_copies[1].start()
    for copy in out_copies:
        copy.wait()


def own_products(owner, pairs, left, slot, left_list, n_left, choices, before, chooses, last):
    bs, n_out = left.shape[-1], pairs.shape[0]
    arrays, plan = [], []
    for step, places, parts in choices:
        at = []
        for part in parts:
            known = [i for i, other in enumerate(arrays) if other is part]
            if not known:
                known = [len(arrays)]
                arrays.append(part)
            at.append(known[0])
        plan.append((step, places, at))
    n_x = sum(part.shape[0] // bs for part in choices[0][2])
    anywhere = pl.BlockSpec(memory_space=pl.ANY)
    smem, operands = [owner, pairs, left_list], [pltpu.with_memory_space_constraint(left, pltpu.HBM), *arrays]
    if before is not None:
        smem.append(before[2])
        operands += before[:2]
    acc_shape, chosen_shape = (n_out + 1, bs, bs), ((slot + 1) * n_x, 2, bs, bs)
    kind = pltpu.VMEM if last else pltpu.HBM
    out_shape, out_specs = [kind(acc_shape, jnp.float32)], [pl.BlockSpec(memory_space=kind)]
    if chooses:
        out_shape += [kind(chosen_shape, jnp.bfloat16), jax.ShapeDtypeStruct((2 * (slot + 1) * n_x,), jnp.int32)]
        out_specs += [pl.BlockSpec(memory_space=kind), SMEM]
    scratch = [pltpu.SMEM((LIST_ROWS, bs), jnp.float32)] * (2 * X_PARTS) + [
        pltpu.VMEM((n_left * bs, bs), jnp.float32),
        pltpu.VMEM((n_x * bs, bs), jnp.float32),
        pltpu.VMEM((n_x * bs, bs), jnp.float32),
        pltpu.SMEM(((KB + 1) * CB,), jnp.int32),
        pltpu.SMEM((RB * CB,), jnp.int32),
        pltpu.SMEM((n_left * CB + 4,), jnp.int32),
        pltpu.SemaphoreType.DMA((5 + 4 * X_PARTS,)),
    ]
    if not last:
        scratch += [pltpu.VMEM(acc_shape, jnp.float32), pltpu.VMEM(chosen_shape, jnp.bfloat16)]
    return pl.pallas_call(
        functools.partial(own_kernel, slot, n_left, n_x, plan, len(arrays), chooses, last),
        in_specs=[SMEM] * len(smem) + [anywhere] * len(operands),
        out_specs=out_specs,
        out_shape=out_shape,
        scratch_shapes=scratch,
        compiler_params=pltpu.CompilerParams(vmem_limit_bytes=OWN_LIMIT),
        cost_estimate=pl.CostEstimate(flops=0, bytes_accessed=2**20, transcendentals=0),
        name="own_products",
    )(*smem, *operands)


OWN_LIMIT = 24 * 2**20
LAST_LIMIT = 24 * 2**20


def their_kernel(n_s, first, last, pairs, late, right_list, left, before, chosen, *refs):
    if last:
        out, acc, left_rows, r_map, o_map, todo, sems = refs
    else:
        acc, left_rows, r_map, o_map, todo, sems = refs
    n_out, bs = pairs.shape[0], left.shape[-1]
    n_left, n_right = left.shape[0] // bs, chosen.shape[0]
    depth = r_map.shape[0] // ((KB + 1) * CB)
    n_x = n_right // depth
    part = left.shape[0] // 4
    fetched = []
    for q in range(4):
        rows = pl.ds(q * part, part)
        fetched.append(pltpu.make_async_copy(left.at[rows], left_rows.at[rows], sems.at[q]))
    for copy in fetched:
        copy.start()
    for m in range(n_out):
        acc[m] = before[m]
    fill_map(o_map, RB * CB, lambda m, d: pairs[m, d], n_out, CB)
    for cell in range(r_map.shape[0]):
        r_map[cell] = -1
    for j in range(n_right):
        r_map[(j // n_x * (KB + 1) + right_list[2 * j]) * CB + right_list[2 * j + 1]] = j
    for copy in fetched:
        copy.wait()

    def left_place(i):
        return late[2 * (first + i)], ((first + i) // n_s * (KB + 1) + late[2 * (first + i) + 1]) * CB

    add_products(
        acc, n_out, bs, (r_map, o_map), todo, left_place, n_left, left_rows, lambda j: (chosen[j, 0], chosen[j, 1])
    )
    if last:
        copies = [pltpu.make_async_copy(acc.at[m], out.at[m], sems.at[4 + m]) for m in range(n_out)]
        for copy in copies:
            copy.start()
        for copy in copies:
            copy.wait()


def their_products(pairs, late, left, first, n_s, before, last):
    bs = left.shape[-1]
    acc, chosen, right_list = before
    n_out, n_left = pairs.shape[0], left.shape[0] // bs
    depth = late.size // (2 * n_s)
    anywhere = pl.BlockSpec(memory_space=pl.ANY)
    return pl.pallas_call(
        functools.partial(their_kernel, n_s, first, last),
        in_specs=[SMEM] * 3 + [anywhere] + [VMEM] * 2,
        out_specs=anywhere if last else VMEM,
        out_shape=jax.ShapeDtypeStruct((n_out, bs, bs) if last else acc.shape, jnp.float32),
        scratch_shapes=([pltpu.VMEM(acc.shape, acc.dtype)] if last else [])
        + [
            pltpu.VMEM(left.shape, left.dtype),
            pltpu.SMEM((depth * (KB + 1) * CB,), jnp.int32),
            pltpu.SMEM((RB * CB,), jnp.int32),
            pltpu.SMEM((n_left * CB + (8 if n_left > 8 else 4),), jnp.int32),
            pltpu.SemaphoreType.DMA((4 + n_out,)),
        ],
        compiler_params=pltpu.CompilerParams(vmem_limit_bytes=LAST_LIMIT),
        cost_estimate=pl.CostEstimate(flops=0, bytes_accessed=2**20, transcendentals=0),
        name="their_products",
    )(pairs, late, right_list, left, acc, chosen)


def per_device(s_blocks, s_list, x_blocks, x_list, c_list, owner):
    length, width = lax.axis_size("loop"), lax.axis_size("bcast")
    pairs, owner = c_list[0, 0], owner[0]
    depth, n_s, bs = s_blocks.shape[2], s_blocks.shape[3], s_blocks.shape[-1]
    n_x = x_blocks.shape[2]
    s_own, x_own = s_blocks.reshape(depth * n_s * bs, bs), x_blocks.reshape(n_x * bs, bs)
    s_own_list, x_own_list = s_list.reshape(depth * n_s, 2), x_list[0, 0]

    swapped = width == 2
    if swapped:
        partner = [(0, 1), (1, 0)]
        their_list = lax.ppermute(s_own_list.reshape(-1), "bcast", partner)
        cuts = (0, depth * n_s - LAST, depth * n_s)
        chunks = [s_own[lo * bs : hi * bs] for lo, hi in zip(cuts, cuts[1:])]
        if LAST:
            chunks[0], their_list = lax.optimization_barrier((chunks[0], their_list))
        came = [lax.ppermute(chunk, "bcast", partner) for chunk in chunks if chunk.size]
    else:
        held = lax.all_gather(s_own, "bcast")
        held_lists = lax.all_gather(s_own_list, "bcast")

    share = n_x // X_PARTS
    everything, *parts = pack(x_own, x_own_list, share)

    def moved(packed, to):
        return [lax.ppermute(part, "loop", [(g, (g + to[g % 4]) % length) for g in range(length)]) for part in packed]

    first = moved(parts, (-1, 1, -1, -3))
    second = moved(first, (1, -1, -3, -1))
    other = moved([everything], (-3, -1, -3, -1))

    choices = [(0, (0, 1, 2, 3), [everything]), (1, (1, 3), first), (1, (0, 2), other)]
    choices += [(2, (0, 1, 2, 3), second), (3, (0,), first), (3, (1, 3), other)]

    def last_choice():
        return (3, (2,), [lax.ppermute(part, "loop", [(g, g - 1) for g in range(3, length, 4)]) for part in second])

    if not swapped:
        choices.append(last_choice())
        total = 0
        for step in range(STEPS):
            piece = lax.dynamic_index_in_dim(held, owner[step], 0, False)
            places = lax.dynamic_index_in_dim(held_lists, owner[step], 0, False)
            fit = [choice for choice in choices if choice[0] == step]
            added = own_products(owner, pairs, piece, step // width, places, n_s, fit, None, False, True)
            total = total + added[0]
        return total[None, None, : pairs.shape[0]]

    sums = None
    for slot in range(depth):
        if slot == 1:
            second[-1], places = lax.optimization_barrier((second[-1], sums[2]))
            sums = (*sums[:2], places)
            choices.append(last_choice())
        fit = [choice for choice in choices if choice[0] // width == slot]
        sums = own_products(owner, pairs, s_own, slot, s_own_list, n_s, fit, sums, True, slot == depth - 1)
    for q, rows in enumerate(came):
        final = q == len(came) - 1
        added = their_products(pairs, their_list, rows, cuts[q], n_s, sums, final)
        sums = (added, *sums[1:])
    return sums[0][None, None]


def solution(mesh):
    return jax.shard_map(
        per_device,
        mesh=mesh,
        in_specs=(
            P("loop", "bcast", None, None, None, None),
            P("loop", "bcast", None, None, None),
            P("loop", "bcast", None, None, None),
            P("loop", "bcast", None, None),
            P("loop", "bcast", None, None),
            P("loop", None),
        ),
        out_specs=P("loop", "bcast", None, None, None),
        check_vma=False,
    )
```

```python
import functools

import jax
import jax.numpy as jnp
from jax import lax
from jax.experimental import pallas as pl
from jax.experimental.pallas import tpu as pltpu
from jax.sharding import PartitionSpec as P

RB = 3
KB = 4
CB = 4
STEPS = 4
LIST_ROWS = 8
SHARES = (4, 8, 12)
X_PARTS = len(SHARES)
FETCH = 5
VMEM = pl.BlockSpec(memory_space=pltpu.VMEM)
SMEM = pl.BlockSpec(memory_space=pltpu.SMEM)


def pack_kernel(cuts, places, x, *refs):
    *targets, sems = refs
    bs = x.shape[-1]
    copies = [
        pltpu.make_async_copy(x.at[pl.ds(first * bs, n * bs)], target.at[pl.ds(0, n * bs)], sems.at[i])
        for i, (target, (first, n)) in enumerate(zip(targets, cuts))
    ]
    for copy in copies:
        copy.start()
    lane = lax.broadcasted_iota(jnp.int32, (LIST_ROWS, bs), 1)
    for target, (first, n) in zip(targets, cuts):
        rows = jnp.zeros((LIST_ROWS, bs), jnp.float32)
        for j in range(n):
            for d in range(2):
                rows = jnp.where(lane == 2 * j + d, places[first + j, d].astype(jnp.float32), rows)
        target[n * bs : n * bs + LIST_ROWS] = rows
    for copy in copies:
        copy.wait()


def pack(x, places):
    n_x, bs = places.shape[0], x.shape[-1]
    ends = [0] + [n_x * share // 12 for share in SHARES]
    cuts = [(0, n_x)] + [(lo, hi - lo) for lo, hi in zip(ends, ends[1:])]
    return pl.pallas_call(
        functools.partial(pack_kernel, cuts),
        in_specs=[SMEM, pl.BlockSpec(memory_space=pl.ANY)],
        out_specs=[VMEM] * len(cuts),
        out_shape=[jax.ShapeDtypeStruct((n * bs + LIST_ROWS, bs), x.dtype) for _, n in cuts],
        scratch_shapes=[pltpu.SemaphoreType.DMA((len(cuts),))],
        compiler_params=pltpu.CompilerParams(vmem_limit_bytes=16 * 2**20),
        cost_estimate=pl.CostEstimate(flops=0, bytes_accessed=2**20, transcendentals=0),
        name="pack",
    )(places, pltpu.with_memory_space_constraint(x, pltpu.HBM))


def halves(values):
    high = values.astype(jnp.bfloat16)
    return high, (values - high.astype(jnp.float32)).astype(jnp.bfloat16)


def dot(left, right):
    return jnp.dot(left, right, preferred_element_type=jnp.float32)


def block(rows, index, bs):
    return rows[pl.ds(pl.multiple_of(index * bs, bs), bs), :]


def fill_map(target, size, read, count, columns):
    for cell in range(size):
        target[cell] = -1
    for entry in range(count):
        target[read(entry, 0) * columns + read(entry, 1)] = entry


def add_products(acc, n_out, bs, maps, todo, left_place, n_left, left, right, arrivals=()):
    r_map, o_map = maps
    unroll = todo.shape[0] - n_left * CB

    def collect(i, count):
        row, base = left_place(i)
        for c in range(CB):
            j, m = r_map[base + c], o_map[row * CB + c]
            todo[count] = (i * 64 + jnp.maximum(j, 0)) * 64 + jnp.maximum(m, 0)
            count = count + ((j >= 0) & (m >= 0)).astype(jnp.int32)
        return count

    def several(q, carry):
        for u in range(unroll):
            code = todo[q * unroll + u]
            i, j, m = code // 4096, (code // 64) % 64, code % 64
            left_high, left_low = halves(block(left, i, bs))
            right_high, right_low = right(j)
            acc[m] += dot(left_high, right_high) + dot(left_high, right_low) + dot(left_low, right_high)
        return carry

    ends, count, entry = [], jnp.int32(0), 0
    for entries, _ in arrivals or [(n_left, None)]:
        count = lax.fori_loop(entry, entry + entries, collect, count)
        entry += entries
        ends.append(count // unroll)
    for u in range(unroll):
        todo[count + u] = n_out
    ends[-1] = (count + unroll - 1) // unroll
    for at, end in enumerate(ends):
        if arrivals:
            arrivals[at][1]()
        lax.fori_loop(ends[at - 1] if at else 0, end, several, 0)


def own_kernel(slot, n_left, n_x, plan, n_arrays, chooses, last, owner, pairs, left_list, *refs):
    refs = list(refs)

    def take(count):
        taken, refs[:count] = refs[:count], []
        return taken

    adds = chooses and slot > 0
    (list_before,) = take(1) if adds else (None,)
    (left,), arrays = take(1), take(n_arrays)
    acc_before, chosen_before = take(2) if adds else (None, None)
    (acc_out,) = take(1)
    chosen_out, chosen_list = take(2) if chooses else (None, None)
    here_lists, there_lists = take(X_PARTS), take(X_PARTS)
    left_rows, here_rows, there_rows, r_map, o_map, todo, sems = take(7)
    acc, chosen = (acc_out, chosen_out) if last else take(2)
    n_out, bs = pairs.shape[0], left.shape[-1]
    place, column = lax.axis_index("loop") % 4, lax.axis_index("bcast")
    mark = slot * n_x if last and chooses else 0

    own_copies = [pltpu.make_async_copy(left.at[pl.ds(slot * n_left * bs, n_left * bs)], left_rows, sems.at[0])]
    if adds:
        own_copies.append(pltpu.make_async_copy(acc_before, acc, sems.at[1]))
        own_copies.append(pltpu.make_async_copy(chosen_before, chosen.at[pl.ds(0, mark)], sems.at[2]))
    for copy in own_copies:
        copy.start()

    def fetch(at, parts, rows, lists):
        copies, entry = [], 0
        for p, array in enumerate(parts):
            right = arrays[array]
            n = right.shape[0] // bs
            target = rows.at[pl.ds(entry * bs, n * bs)]
            entry += n
            copies.append(pltpu.make_async_copy(right.at[pl.ds(0, n * bs)], target, sems.at[at + 2 * p]))
            listed = right.at[pl.ds(n * bs, LIST_ROWS)]
            copies.append(pltpu.make_async_copy(listed, lists[p], sems.at[at + 2 * p + 1]))
        return copies

    def copies_of(parts, here):
        if here:
            return fetch(6, parts, here_rows, here_lists)
        return fetch(6 + 2 * X_PARTS, parts, there_rows, there_lists)

    def place_in(lists, parts):
        at = [(p, j) for p, array in enumerate(parts) for j in range(arrays[array].shape[0] // bs)]
        return lambda j, d: lists[at[j][0]][0, 2 * at[j][1] + d].astype(jnp.int32)

    def each(then):
        for step, places, parts in plan:
            applies = functools.reduce(jnp.logical_or, [place == value for value in places])
            mine = owner[step] == column if chooses else True
            pl.when(applies & mine)(functools.partial(then, parts, True))
            if chooses:
                pl.when(applies & jnp.logical_not(mine))(functools.partial(then, parts, False))

    def start(parts, here):
        for copy in copies_of(parts, here):
            copy.start()

    def land(wanted, parts, here):
        if here != wanted:
            return
        for copy in copies_of(parts, here):
            copy.wait()
        if here:
            fill_map(r_map, KB * CB, place_in(here_lists, parts), n_x, CB)
            return
        read = place_in(there_lists, parts)
        for j in range(n_x):
            for d in range(2):
                chosen_list[2 * (slot * n_x + j) + d] = read(j, d)

    def left_place(i):
        return left_list[slot * n_left + i, 0], left_list[slot * n_left + i, 1] * CB

    each(start)
    fill_map(o_map, RB * CB, lambda m, d: pairs[m, d], n_out, CB)
    if adds:
        for q in range(2 * slot * n_x):
            chosen_list[q] = list_before[q]
    else:
        acc[...] = jnp.zeros_like(acc)
    each(functools.partial(land, True))
    for copy in own_copies:
        copy.wait()
    add_products(
        acc, n_out, bs, (r_map, o_map), todo, left_place, n_left, left_rows, lambda j: halves(block(here_rows, j, bs))
    )
    if not chooses:
        return
    out_copies = []
    if not last:
        out_copies.append(pltpu.make_async_copy(acc, acc_out, sems.at[3]))
        out_copies[0].start()
    each(functools.partial(land, False))

    def split(j, carry):
        chosen[mark + j, 0], chosen[mark + j, 1] = halves(block(there_rows, j, bs))
        return carry

    for q, (lo, hi) in enumerate(((0, n_x // 2), (n_x // 2, n_x))):
        lax.fori_loop(lo, hi, split, 0)
        if not last:
            rows = pl.ds(lo, hi - lo)
            out_copies.append(pltpu.make_async_copy(chosen.at[rows], chosen_out.at[rows], sems.at[4 + q]))
            out_copies[-1].start()
    for copy in out_copies:
        copy.wait()


def own_products(owner, pairs, left, slot, left_list, n_left, choices, before, chooses, last):
    bs, n_out = left.shape[-1], pairs.shape[0]
    arrays, plan = [], []
    for step, places, parts in choices:
        at = []
        for part in parts:
            known = [i for i, other in enumerate(arrays) if other is part]
            if not known:
                known = [len(arrays)]
                arrays.append(part)
            at.append(known[0])
        plan.append((step, places, at))
    n_x = sum(part.shape[0] // bs for part in choices[0][2])
    anywhere = pl.BlockSpec(memory_space=pl.ANY)
    smem = [owner, pairs, left_list]
    operands = [pltpu.with_memory_space_constraint(rows, pltpu.HBM) for rows in (left, *arrays)]
    if before is not None:
        smem.append(before[2])
        operands += [pltpu.with_memory_space_constraint(one, pltpu.HBM) for one in before[:2]]
    acc_shape, chosen_shape = (n_out + 1, bs, bs), ((slot + 1) * n_x, 2, bs, bs)
    kind = pltpu.VMEM if last else pltpu.HBM
    out_shape, out_specs = [kind(acc_shape, jnp.float32)], [pl.BlockSpec(memory_space=kind)]
    if chooses:
        out_shape += [kind(chosen_shape, jnp.bfloat16), jax.ShapeDtypeStruct((2 * (slot + 1) * n_x,), jnp.int32)]
        out_specs += [pl.BlockSpec(memory_space=kind), SMEM]
    scratch = [pltpu.SMEM((LIST_ROWS, bs), jnp.float32)] * (2 * X_PARTS) + [
        pltpu.VMEM((n_left * bs, bs), jnp.float32),
        pltpu.VMEM((n_x * bs, bs), jnp.float32),
        pltpu.VMEM((n_x * bs, bs), jnp.float32),
        pltpu.SMEM(((KB + 1) * CB,), jnp.int32),
        pltpu.SMEM((RB * CB,), jnp.int32),
        pltpu.SMEM((n_left * CB + 4,), jnp.int32),
        pltpu.SemaphoreType.DMA((6 + 4 * X_PARTS,)),
    ]
    if not last:
        scratch += [pltpu.VMEM(acc_shape, jnp.float32), pltpu.VMEM(chosen_shape, jnp.bfloat16)]
    return pl.pallas_call(
        functools.partial(own_kernel, slot, n_left, n_x, plan, len(arrays), chooses, last),
        in_specs=[SMEM] * len(smem) + [anywhere] * len(operands),
        out_specs=out_specs,
        out_shape=out_shape,
        scratch_shapes=scratch,
        compiler_params=pltpu.CompilerParams(vmem_limit_bytes=OWN_LIMIT),
        cost_estimate=pl.CostEstimate(flops=0, bytes_accessed=2**20, transcendentals=0),
        name="own_products",
    )(*smem, *operands)


OWN_LIMIT = 24 * 2**20
LAST_LIMIT = 24 * 2**20


def last_kernel(n_s, pairs, late, right_list, left, before, chosen, out, acc, left_rows, r_map, o_map, todo, sems):
    n_out, bs = pairs.shape[0], left.shape[-1]
    n_right = chosen.shape[0]
    depth = left.shape[0] // (n_s * bs)
    n_x = n_right // depth
    n_left = left.shape[0] // bs
    arrivals = []
    for q, (lo, hi) in enumerate(zip(range(0, n_left, FETCH), [*range(FETCH, n_left, FETCH), n_left])):
        rows = pl.ds(lo * bs, (hi - lo) * bs)
        copy = pltpu.make_async_copy(left.at[rows], left_rows.at[rows], sems.at[n_out + q])
        copy.start()
        arrivals.append((hi - lo, copy.wait))
    fill_map(o_map, RB * CB, lambda m, d: pairs[m, d], n_out, CB)
    for cell in range(r_map.shape[0]):
        r_map[cell] = -1
    for j in range(n_right):
        r_map[(j // n_x * (KB + 1) + right_list[2 * j]) * CB + right_list[2 * j + 1]] = j
    for m in range(n_out):
        acc[m] = before[m]

    def left_place(i):
        return late[2 * i], (i // n_s * (KB + 1) + late[2 * i + 1]) * CB

    add_products(
        acc, n_out, bs, (r_map, o_map), todo, left_place, n_left, left_rows, lambda j: (chosen[j, 0], chosen[j, 1]), arrivals
    )
    copies = [pltpu.make_async_copy(acc.at[m], out.at[m], sems.at[m]) for m in range(n_out)]
    for copy in copies:
        copy.start()
    for copy in copies:
        copy.wait()


def last_products(pairs, late, left, n_s, acc, chosen, right_list):
    bs = left.shape[-1]
    n_out, depth = pairs.shape[0], left.shape[0] // (n_s * bs)
    anywhere = pl.BlockSpec(memory_space=pl.ANY)
    return pl.pallas_call(
        functools.partial(last_kernel, n_s),
        in_specs=[SMEM] * 3 + [anywhere] + [VMEM] * 2,
        out_specs=anywhere,
        out_shape=jax.ShapeDtypeStruct((n_out, bs, bs), jnp.float32),
        scratch_shapes=[
            pltpu.VMEM(acc.shape, acc.dtype),
            pltpu.VMEM(left.shape, left.dtype),
            pltpu.SMEM((depth * (KB + 1) * CB,), jnp.int32),
            pltpu.SMEM((RB * CB,), jnp.int32),
            pltpu.SMEM((depth * n_s * CB + 8,), jnp.int32),
            pltpu.SemaphoreType.DMA((n_out + pl.cdiv(depth * n_s, FETCH),)),
        ],
        compiler_params=pltpu.CompilerParams(vmem_limit_bytes=LAST_LIMIT),
        cost_estimate=pl.CostEstimate(flops=0, bytes_accessed=2**20, transcendentals=0),
        name="last_products",
    )(pairs, late, right_list, pltpu.with_memory_space_constraint(left, pltpu.HBM), acc, chosen)


def per_device(s_blocks, s_list, x_blocks, x_list, c_list, owner):
    length, width = lax.axis_size("loop"), lax.axis_size("bcast")
    pairs, owner = c_list[0, 0], owner[0]
    depth, n_s, bs = s_blocks.shape[2], s_blocks.shape[3], s_blocks.shape[-1]
    n_x = x_blocks.shape[2]
    s_own, x_own = s_blocks.reshape(depth * n_s * bs, bs), x_blocks.reshape(n_x * bs, bs)
    s_own_list, x_own_list = s_list.reshape(depth * n_s, 2), x_list[0, 0]

    swapped = width == 2
    if swapped:
        partner = [(0, 1), (1, 0)]
        came = lax.ppermute(s_own, "bcast", partner)
        their_list = lax.ppermute(s_own_list.reshape(-1), "bcast", partner)
    else:
        held = lax.all_gather(s_own, "bcast")
        held_lists = lax.all_gather(s_own_list, "bcast")

    everything, *parts = pack(x_own, x_own_list)

    def moved(packed, to):
        return [lax.ppermute(part, "loop", [(g, (g + to[g % 4]) % length) for g in range(length)]) for part in packed]

    first = moved(parts, (-1, 1, -1, -3))
    second = moved(first, (1, -1, -3, -1))
    other = moved([everything], (-3, -1, -3, -1))

    choices = [(0, (0, 1, 2, 3), [everything]), (1, (1, 3), first), (1, (0, 2), other)]
    choices += [(2, (0, 1, 2, 3), second), (3, (0,), first), (3, (1, 3), other)]

    def last_choice():
        return (3, (2,), [lax.ppermute(part, "loop", [(g, g - 1) for g in range(3, length, 4)]) for part in second])

    if not swapped:
        choices.append(last_choice())
        total = 0
        for step in range(STEPS):
            piece = lax.dynamic_index_in_dim(held, owner[step], 0, False)
            places = lax.dynamic_index_in_dim(held_lists, owner[step], 0, False)
            fit = [choice for choice in choices if choice[0] == step]
            added = own_products(owner, pairs, piece, step // width, places, n_s, fit, None, False, True)
            total = total + added[0]
        return total[None, None, : pairs.shape[0]]

    sums = None
    for slot in range(depth):
        if slot == 1:
            second[-1], places = lax.optimization_barrier((second[-1], sums[2]))
            sums = (*sums[:2], places)
            choices.append(last_choice())
        fit = [choice for choice in choices if choice[0] // width == slot]
        sums = own_products(owner, pairs, s_own, slot, s_own_list, n_s, fit, sums, True, slot == depth - 1)
    return last_products(pairs, their_list, came, n_s, *sums)[None, None]


def solution(mesh):
    return jax.shard_map(
        per_device,
        mesh=mesh,
        in_specs=(
            P("loop", "bcast", None, None, None, None),
            P("loop", "bcast", None, None, None),
            P("loop", "bcast", None, None, None),
            P("loop", "bcast", None, None),
            P("loop", "bcast", None, None),
            P("loop", None),
        ),
        out_specs=P("loop", "bcast", None, None, None),
        check_vma=False,
    )
```

```python
import functools

import jax
import jax.numpy as jnp
from jax import lax
from jax.experimental import pallas as pl
from jax.experimental.pallas import tpu as pltpu
from jax.sharding import PartitionSpec as P

RB = 3
KB = 4
CB = 4
STEPS = 4
LIST_ROWS = 8
SHARES = (4, 8, 12)
X_PARTS = len(SHARES)
FETCH = 5
WIDE, NARROW = 8, 4
VMEM = pl.BlockSpec(memory_space=pltpu.VMEM)
SMEM = pl.BlockSpec(memory_space=pltpu.SMEM)


def pack_kernel(cuts, places, x, *refs):
    *targets, sems = refs
    bs = x.shape[-1]
    copies = [
        pltpu.make_async_copy(x.at[pl.ds(first * bs, n * bs)], target.at[pl.ds(0, n * bs)], sems.at[i])
        for i, (target, (first, n)) in enumerate(zip(targets, cuts))
    ]
    for copy in copies:
        copy.start()
    lane = lax.broadcasted_iota(jnp.int32, (LIST_ROWS, bs), 1)
    for target, (first, n) in zip(targets, cuts):
        rows = jnp.zeros((LIST_ROWS, bs), jnp.float32)
        for j in range(n):
            for d in range(2):
                rows = jnp.where(lane == 2 * j + d, places[first + j, d].astype(jnp.float32), rows)
        target[n * bs : n * bs + LIST_ROWS] = rows
    for copy in copies:
        copy.wait()


def pack(x, places):
    n_x, bs = places.shape[0], x.shape[-1]
    ends = [0] + [n_x * share // 12 for share in SHARES]
    cuts = [(0, n_x)] + [(lo, hi - lo) for lo, hi in zip(ends, ends[1:])]
    return pl.pallas_call(
        functools.partial(pack_kernel, cuts),
        in_specs=[SMEM, pl.BlockSpec(memory_space=pl.ANY)],
        out_specs=[VMEM] * len(cuts),
        out_shape=[jax.ShapeDtypeStruct((n * bs + LIST_ROWS, bs), x.dtype) for _, n in cuts],
        scratch_shapes=[pltpu.SemaphoreType.DMA((len(cuts),))],
        compiler_params=pltpu.CompilerParams(vmem_limit_bytes=16 * 2**20),
        cost_estimate=pl.CostEstimate(flops=0, bytes_accessed=2**20, transcendentals=0),
        name="pack",
    )(places, pltpu.with_memory_space_constraint(x, pltpu.HBM))


def halves(values):
    high = values.astype(jnp.bfloat16)
    return high, (values - high.astype(jnp.float32)).astype(jnp.bfloat16)


def dot(left, right):
    return jnp.dot(left, right, preferred_element_type=jnp.float32)


def block(rows, index, bs):
    return rows[pl.ds(pl.multiple_of(index * bs, bs), bs), :]


def fill_map(target, size, read, count, columns):
    for cell in range(size):
        target[cell] = -1
    for entry in range(count):
        target[read(entry, 0) * columns + read(entry, 1)] = entry


def add_products(acc, n_out, bs, maps, todo, left_place, n_left, left, right, arrivals=()):
    r_map, o_map = maps
    unroll = todo.shape[0] - n_left * CB

    def collect(i, count):
        row, base = left_place(i)
        for c in range(CB):
            j, m = r_map[base + c], o_map[row * CB + c]
            todo[count] = (i * 64 + jnp.maximum(j, 0)) * 64 + jnp.maximum(m, 0)
            count = count + ((j >= 0) & (m >= 0)).astype(jnp.int32)
        return count

    def several(q, carry):
        for u in range(unroll):
            code = todo[q * unroll + u]
            i, j, m = code // 4096, (code // 64) % 64, code % 64
            left_high, left_low = halves(block(left, i, bs))
            right_high, right_low = right(j)
            acc[m] += dot(left_high, right_high) + dot(left_high, right_low) + dot(left_low, right_high)
        return carry

    ends, count, entry = [], jnp.int32(0), 0
    for entries, _ in arrivals or [(n_left, None)]:
        count = lax.fori_loop(entry, entry + entries, collect, count)
        entry += entries
        ends.append(count // unroll)
    for u in range(unroll):
        todo[count + u] = n_out
    ends[-1] = (count + unroll - 1) // unroll
    for at, end in enumerate(ends):
        if arrivals:
            arrivals[at][1]()
        lax.fori_loop(ends[at - 1] if at else 0, end, several, 0)


def own_kernel(slot, n_left, n_x, plan, n_arrays, chooses, last, owner, pairs, left_list, *refs):
    refs = list(refs)

    def take(count):
        taken, refs[:count] = refs[:count], []
        return taken

    adds = chooses and slot > 0
    (list_before,) = take(1) if adds else (None,)
    (left,), arrays = take(1), take(n_arrays)
    acc_before, chosen_before = take(2) if adds else (None, None)
    (acc_out,) = take(1)
    chosen_out, chosen_list = take(2) if chooses else (None, None)
    here_lists, there_lists = take(X_PARTS), take(X_PARTS)
    left_rows, here_rows, there_rows, r_map, o_map, todo, sems = take(7)
    acc, chosen = (acc_out, chosen_out) if last else take(2)
    n_out, bs = pairs.shape[0], left.shape[-1]
    place, column = lax.axis_index("loop") % 4, lax.axis_index("bcast")
    mark = slot * n_x if last and chooses else 0

    half = n_left // 2
    margins = []
    for q, (lo, n) in enumerate(((0, half), (half, n_left - half))):
        source = left.at[pl.ds((slot * n_left + lo) * bs, n * bs)]
        margins.append(pltpu.make_async_copy(source, left_rows.at[pl.ds(lo * bs, n * bs)], sems.at[q]))
    if adds:
        sums_copy = pltpu.make_async_copy(acc_before, acc, sems.at[2])
        chosen_copy = pltpu.make_async_copy(chosen_before, chosen.at[pl.ds(0, mark)], sems.at[3])

    def fetch(at, parts, rows, lists):
        copies, entry = [], 0
        for p, array in enumerate(parts):
            right = arrays[array]
            n = right.shape[0] // bs
            target = rows.at[pl.ds(entry * bs, n * bs)]
            entry += n
            copies.append(pltpu.make_async_copy(right.at[pl.ds(0, n * bs)], target, sems.at[at + 2 * p]))
            listed = right.at[pl.ds(n * bs, LIST_ROWS)]
            copies.append(pltpu.make_async_copy(listed, lists[p], sems.at[at + 2 * p + 1]))
        return copies

    def copies_of(parts, here):
        if here:
            return fetch(7, parts, here_rows, here_lists)
        return fetch(7 + 2 * X_PARTS, parts, there_rows, there_lists)

    def place_in(lists, parts):
        at = [(p, j) for p, array in enumerate(parts) for j in range(arrays[array].shape[0] // bs)]
        return lambda j, d: lists[at[j][0]][0, 2 * at[j][1] + d].astype(jnp.int32)

    def each(then):
        for step, places, parts in plan:
            applies = functools.reduce(jnp.logical_or, [place == value for value in places])
            mine = owner[step] == column if chooses else True
            pl.when(applies & mine)(functools.partial(then, parts, True))
            if chooses:
                pl.when(applies & jnp.logical_not(mine))(functools.partial(then, parts, False))

    def start(wanted, parts, here):
        if here == wanted:
            for copy in copies_of(parts, here):
                copy.start()

    def land(wanted, parts, here):
        if here != wanted:
            return
        for copy in copies_of(parts, here):
            copy.wait()
        if here:
            fill_map(r_map, KB * CB, place_in(here_lists, parts), n_x, CB)
            return
        read = place_in(there_lists, parts)
        for j in range(n_x):
            for d in range(2):
                chosen_list[2 * (slot * n_x + j) + d] = read(j, d)

    def left_place(i):
        return left_list[slot * n_left + i, 0], left_list[slot * n_left + i, 1] * CB

    margins[0].start()
    each(functools.partial(start, True))
    if adds:
        sums_copy.start()
    margins[1].start()
    fill_map(o_map, RB * CB, lambda m, d: pairs[m, d], n_out, CB)
    if adds:
        for q in range(2 * slot * n_x):
            chosen_list[q] = list_before[q]
    else:
        acc[...] = jnp.zeros_like(acc)
    each(functools.partial(land, True))
    if adds:
        sums_copy.wait()
        chosen_copy.start()
    if chooses:
        each(functools.partial(start, False))
    arrivals = [(half, margins[0].wait), (n_left - half, margins[1].wait)]
    add_products(
        acc, n_out, bs, (r_map, o_map), todo, left_place, n_left, left_rows, lambda j: halves(block(here_rows, j, bs)), arrivals
    )
    if adds:
        chosen_copy.wait()
    if not chooses:
        return
    out_copies = []
    if not last:
        out_copies.append(pltpu.make_async_copy(acc, acc_out, sems.at[4]))
        out_copies[0].start()
    each(functools.partial(land, False))

    def split(j, carry):
        chosen[mark + j, 0], chosen[mark + j, 1] = halves(block(there_rows, j, bs))
        return carry

    for q, (lo, hi) in enumerate(((0, n_x // 2), (n_x // 2, n_x))):
        lax.fori_loop(lo, hi, split, 0)
        if not last:
            rows = pl.ds(lo, hi - lo)
            out_copies.append(pltpu.make_async_copy(chosen.at[rows], chosen_out.at[rows], sems.at[5 + q]))
            out_copies[-1].start()
    for copy in out_copies:
        copy.wait()


def own_products(owner, pairs, left, slot, left_list, n_left, choices, before, chooses, last):
    bs, n_out = left.shape[-1], pairs.shape[0]
    arrays, plan = [], []
    for step, places, parts in choices:
        at = []
        for part in parts:
            known = [i for i, other in enumerate(arrays) if other is part]
            if not known:
                known = [len(arrays)]
                arrays.append(part)
            at.append(known[0])
        plan.append((step, places, at))
    n_x = sum(part.shape[0] // bs for part in choices[0][2])
    anywhere = pl.BlockSpec(memory_space=pl.ANY)
    smem = [owner, pairs, left_list]
    operands = [pltpu.with_memory_space_constraint(rows, pltpu.HBM) for rows in (left, *arrays)]
    if before is not None:
        smem.append(before[2])
        operands += [pltpu.with_memory_space_constraint(one, pltpu.HBM) for one in before[:2]]
    acc_shape, chosen_shape = (n_out + 1, bs, bs), ((slot + 1) * n_x, 2, bs, bs)
    kind = pltpu.VMEM if last else pltpu.HBM
    out_shape, out_specs = [kind(acc_shape, jnp.float32)], [pl.BlockSpec(memory_space=kind)]
    if chooses:
        out_shape += [kind(chosen_shape, jnp.bfloat16), jax.ShapeDtypeStruct((2 * (slot + 1) * n_x,), jnp.int32)]
        out_specs += [pl.BlockSpec(memory_space=kind), SMEM]
    scratch = [pltpu.SMEM((LIST_ROWS, bs), jnp.float32)] * (2 * X_PARTS) + [
        pltpu.VMEM((n_left * bs, bs), jnp.float32),
        pltpu.VMEM((n_x * bs, bs), jnp.float32),
        pltpu.VMEM((n_x * bs, bs), jnp.float32),
        pltpu.SMEM(((KB + 1) * CB,), jnp.int32),
        pltpu.SMEM((RB * CB,), jnp.int32),
        pltpu.SMEM((n_left * CB + 4,), jnp.int32),
        pltpu.SemaphoreType.DMA((7 + 4 * X_PARTS,)),
    ]
    if not last:
        scratch += [pltpu.VMEM(acc_shape, jnp.float32), pltpu.VMEM(chosen_shape, jnp.bfloat16)]
    return pl.pallas_call(
        functools.partial(own_kernel, slot, n_left, n_x, plan, len(arrays), chooses, last),
        in_specs=[SMEM] * len(smem) + [anywhere] * len(operands),
        out_specs=out_specs,
        out_shape=out_shape,
        scratch_shapes=scratch,
        compiler_params=pltpu.CompilerParams(vmem_limit_bytes=OWN_LIMIT),
        cost_estimate=pl.CostEstimate(flops=0, bytes_accessed=2**20, transcendentals=0),
        name="own_products",
    )(*smem, *operands)


OWN_LIMIT = 24 * 2**20
LAST_LIMIT = 24 * 2**20


def last_kernel(n_s, pairs, late, right_list, left, before, chosen, out, acc, left_rows, maps, todo, sems):
    r_map, o_map, l_map = maps
    n_out, bs = pairs.shape[0], left.shape[-1]
    n_right, n_left = chosen.shape[0], left.shape[0] // bs
    depth = n_left // n_s
    n_x = n_right // depth
    starts = list(range(0, n_left, FETCH))
    fetched = []
    for q, lo in enumerate(starts):
        rows = pl.ds(lo * bs, min(FETCH, n_left - lo) * bs)
        fetched.append(pltpu.make_async_copy(left.at[rows], left_rows.at[rows], sems.at[n_out + q]))
        fetched[q].start()
    fill_map(o_map, RB * CB, lambda m, d: pairs[m, d], n_out, CB)
    for cell in range(r_map.shape[0]):
        r_map[cell] = -1
    for j in range(n_right):
        r_map[(j // n_x * (KB + 1) + right_list[2 * j]) * CB + right_list[2 * j + 1]] = j
    for m in range(n_out):
        acc[m] = before[m]

    def note(count, i, j, m):
        todo[count] = (i * 64 + jnp.maximum(j, 0)) * 64 + jnp.maximum(m, 0)
        return count + ((i >= 0) & (j >= 0) & (m >= 0)).astype(jnp.int32)

    def collect(i, count):
        row, base = late[2 * i], (i // n_s * (KB + 1) + late[2 * i + 1]) * CB
        for c in range(CB):
            count = note(count, i, r_map[base + c], o_map[row * CB + c])
        return count

    count, ends = jnp.int32(0), []
    for lo, hi in zip(starts, starts[1:]):
        count = lax.fori_loop(lo, hi, collect, count)
        ends.append(count // WIDE)
    ordered = count
    slots = range(starts[-1] // n_s, depth)
    for cell in range(l_map.shape[0]):
        l_map[cell] = -1
    for i in range(starts[-1], n_left):
        l_map[(i // n_s - slots[0]) * RB * KB + late[2 * i] * KB + late[2 * i + 1]] = i

    def gather(m, count):
        row, c = pairs[m, 0], pairs[m, 1]
        for slot in slots:
            for k in range(KB):
                i = l_map[(slot - slots[0]) * RB * KB + row * KB + k]
                count = note(count, i, r_map[(slot * (KB + 1) + k) * CB + c], m)
        return count

    count = lax.fori_loop(0, n_out, gather, count)
    for u in range(2 * NARROW):
        todo[count + u] = n_out

    def product(code):
        i, j, m = code // 4096, (code // 64) % 64, code % 64
        left_high, left_low = halves(block(left_rows, i, bs))
        high, low = chosen[j, 0], chosen[j, 1]
        acc[m] += dot(left_high, high) + dot(left_high, low) + dot(left_low, high)

    def several(q, carry):
        for u in range(WIDE):
            product(todo[q * WIDE + u])
        return carry

    def send(m, carry):
        pltpu.make_async_copy(acc.at[m], out.at[m], sems.at[m]).start()
        return carry

    def several_and_send(q, sent):
        for u in range(NARROW):
            product(todo[q * NARROW + u])
        following = (q + 1) * NARROW
        done = jnp.where(following >= ordered, todo[following] % 64, sent)
        lax.fori_loop(sent, done, send, 0)
        return done

    at = 0
    for copy, end in zip(fetched, ends):
        copy.wait()
        lax.fori_loop(at, end, several, 0)
        at = end
    fetched[-1].wait()
    sent = lax.fori_loop(at * (WIDE // NARROW), (count + NARROW - 1) // NARROW, several_and_send, jnp.int32(0))
    lax.fori_loop(sent, n_out, send, 0)
    for m in range(n_out):
        pltpu.make_async_copy(acc.at[m], out.at[m], sems.at[m]).wait()


def last_products(pairs, late, left, n_s, acc, chosen, right_list):
    bs = left.shape[-1]
    n_out, depth = pairs.shape[0], left.shape[0] // (n_s * bs)
    anywhere = pl.BlockSpec(memory_space=pl.ANY)
    return pl.pallas_call(
        functools.partial(last_kernel, n_s),
        in_specs=[SMEM] * 3 + [anywhere] + [VMEM] * 2,
        out_specs=anywhere,
        out_shape=jax.ShapeDtypeStruct((n_out, bs, bs), jnp.float32),
        scratch_shapes=[
            pltpu.VMEM(acc.shape, acc.dtype),
            pltpu.VMEM(left.shape, left.dtype),
            [pltpu.SMEM((size,), jnp.int32) for size in (depth * (KB + 1) * CB, RB * CB, depth * RB * KB)],
            pltpu.SMEM((depth * n_s * CB + 2 * NARROW,), jnp.int32),
            pltpu.SemaphoreType.DMA((n_out + pl.cdiv(depth * n_s, FETCH),)),
        ],
        compiler_params=pltpu.CompilerParams(vmem_limit_bytes=LAST_LIMIT),
        cost_estimate=pl.CostEstimate(flops=0, bytes_accessed=2**20, transcendentals=0),
        name="last_products",
    )(pairs, late, right_list, pltpu.with_memory_space_constraint(left, pltpu.HBM), acc, chosen)


def per_device(s_blocks, s_list, x_blocks, x_list, c_list, owner):
    length, width = lax.axis_size("loop"), lax.axis_size("bcast")
    pairs, owner = c_list[0, 0], owner[0]
    depth, n_s, bs = s_blocks.shape[2], s_blocks.shape[3], s_blocks.shape[-1]
    n_x = x_blocks.shape[2]
    s_own, x_own = s_blocks.reshape(depth * n_s * bs, bs), x_blocks.reshape(n_x * bs, bs)
    s_own_list, x_own_list = s_list.reshape(depth * n_s, 2), x_list[0, 0]

    swapped = width == 2
    if swapped:
        partner = [(0, 1), (1, 0)]
        came = lax.ppermute(s_own, "bcast", partner)
        their_list = lax.ppermute(s_own_list.reshape(-1), "bcast", partner)
    else:
        held = lax.all_gather(s_own, "bcast")
        held_lists = lax.all_gather(s_own_list, "bcast")

    everything, *parts = pack(x_own, x_own_list)

    def moved(packed, to):
        return [lax.ppermute(part, "loop", [(g, (g + to[g % 4]) % length) for g in range(length)]) for part in packed]

    first = moved(parts, (-1, 1, -1, -3))
    second = moved(first, (1, -1, -3, -1))
    other = moved([everything], (-3, -1, -3, -1))

    choices = [(0, (0, 1, 2, 3), [everything]), (1, (1, 3), first), (1, (0, 2), other)]
    choices += [(2, (0, 1, 2, 3), second), (3, (0,), first), (3, (1, 3), other)]

    def last_choice():
        return (3, (2,), [lax.ppermute(part, "loop", [(g, g - 1) for g in range(3, length, 4)]) for part in second])

    if not swapped:
        choices.append(last_choice())
        total = 0
        for step in range(STEPS):
            piece = lax.dynamic_index_in_dim(held, owner[step], 0, False)
            places = lax.dynamic_index_in_dim(held_lists, owner[step], 0, False)
            fit = [choice for choice in choices if choice[0] == step]
            added = own_products(owner, pairs, piece, step // width, places, n_s, fit, None, False, True)
            total = total + added[0]
        return total[None, None, : pairs.shape[0]]

    sums = None
    for slot in range(depth):
        if slot == 1:
            second[-1], places = lax.optimization_barrier((second[-1], sums[2]))
            sums = (*sums[:2], places)
            choices.append(last_choice())
        fit = [choice for choice in choices if choice[0] // width == slot]
        sums = own_products(owner, pairs, s_own, slot, s_own_list, n_s, fit, sums, True, slot == depth - 1)
    return last_products(pairs, their_list, came, n_s, *sums)[None, None]


def solution(mesh):
    return jax.shard_map(
        per_device,
        mesh=mesh,
        in_specs=(
            P("loop", "bcast", None, None, None, None),
            P("loop", "bcast", None, None, None),
            P("loop", "bcast", None, None, None),
            P("loop", "bcast", None, None),
            P("loop", "bcast", None, None),
            P("loop", None),
        ),
        out_specs=P("loop", "bcast", None, None, None),
        check_vma=False,
    )
```

```python
import functools

import jax
import jax.numpy as jnp
from jax import lax
from jax.experimental import pallas as pl
from jax.experimental.pallas import tpu as pltpu
from jax.sharding import PartitionSpec as P

RB = 3
KB = 4
CB = 4
STEPS = 4
LIST_ROWS = 8
SHARES = (4, 8, 12)
X_PARTS = len(SHARES)
FETCH = 5
WIDE, NARROW = 8, 4
VMEM = pl.BlockSpec(memory_space=pltpu.VMEM)
SMEM = pl.BlockSpec(memory_space=pltpu.SMEM)


def pack_kernel(cuts, places, x, *refs):
    *targets, sems = refs
    bs = x.shape[-1]
    copies = [
        pltpu.make_async_copy(x.at[pl.ds(first * bs, n * bs)], target.at[pl.ds(0, n * bs)], sems.at[i])
        for i, (target, (first, n)) in enumerate(zip(targets, cuts))
    ]
    for copy in copies:
        copy.start()
    lane = lax.broadcasted_iota(jnp.int32, (LIST_ROWS, bs), 1)
    for target, (first, n) in zip(targets, cuts):
        rows = jnp.zeros((LIST_ROWS, bs), jnp.float32)
        for j in range(n):
            for d in range(2):
                rows = jnp.where(lane == 2 * j + d, places[first + j, d].astype(jnp.float32), rows)
        target[n * bs : n * bs + LIST_ROWS] = rows
    for copy in copies:
        copy.wait()


def pack(x, places):
    n_x, bs = places.shape[0], x.shape[-1]
    ends = [0] + [n_x * share // 12 for share in SHARES]
    cuts = [(0, n_x)] + [(lo, hi - lo) for lo, hi in zip(ends, ends[1:])]
    return pl.pallas_call(
        functools.partial(pack_kernel, cuts),
        in_specs=[SMEM, pl.BlockSpec(memory_space=pl.ANY)],
        out_specs=[VMEM] * len(cuts),
        out_shape=[jax.ShapeDtypeStruct((n * bs + LIST_ROWS, bs), x.dtype) for _, n in cuts],
        scratch_shapes=[pltpu.SemaphoreType.DMA((len(cuts),))],
        compiler_params=pltpu.CompilerParams(vmem_limit_bytes=16 * 2**20),
        cost_estimate=pl.CostEstimate(flops=0, bytes_accessed=2**20, transcendentals=0),
        name="pack",
    )(places, pltpu.with_memory_space_constraint(x, pltpu.HBM))


def halves(values):
    high = values.astype(jnp.bfloat16)
    return high, (values - high.astype(jnp.float32)).astype(jnp.bfloat16)


def dot(left, right):
    return jnp.dot(left, right, preferred_element_type=jnp.float32)


def block(rows, index, bs):
    return rows[pl.ds(pl.multiple_of(index * bs, bs), bs), :]


def fill_map(target, size, read, count, columns):
    for cell in range(size):
        target[cell] = -1
    for entry in range(count):
        target[read(entry, 0) * columns + read(entry, 1)] = entry


def add_products(acc, n_out, bs, maps, todo, left_place, n_left, left, right, arrivals=()):
    r_map, o_map = maps
    unroll = todo.shape[0] - n_left * CB

    def collect(i, count):
        row, base = left_place(i)
        for c in range(CB):
            j, m = r_map[base + c], o_map[row * CB + c]
            todo[count] = (i * 64 + jnp.maximum(j, 0)) * 64 + jnp.maximum(m, 0)
            count = count + ((j >= 0) & (m >= 0)).astype(jnp.int32)
        return count

    def several(q, carry):
        for u in range(unroll):
            code = todo[q * unroll + u]
            i, j, m = code // 4096, (code // 64) % 64, code % 64
            left_high, left_low = halves(block(left, i, bs))
            right_high, right_low = right(j)
            acc[m] += dot(left_high, right_high) + dot(left_high, right_low) + dot(left_low, right_high)
        return carry

    ends, count, entry = [], jnp.int32(0), 0
    for entries, _ in arrivals or [(n_left, None)]:
        count = lax.fori_loop(entry, entry + entries, collect, count)
        entry += entries
        ends.append(count // unroll)
    for u in range(unroll):
        todo[count + u] = n_out
    ends[-1] = (count + unroll - 1) // unroll
    for at, end in enumerate(ends):
        if arrivals:
            arrivals[at][1]()
        lax.fori_loop(ends[at - 1] if at else 0, end, several, 0)


def own_kernel(slot, n_left, n_x, plan, n_arrays, chooses, last, owner, pairs, left_list, *refs):
    refs = list(refs)

    def take(count):
        taken, refs[:count] = refs[:count], []
        return taken

    adds = chooses and slot > 0
    (list_before,) = take(1) if adds else (None,)
    (left,), arrays = take(1), take(n_arrays)
    acc_before, chosen_before = take(2) if adds else (None, None)
    (acc_out,) = take(1)
    chosen_out, chosen_list = take(2) if chooses else (None, None)
    here_lists, there_lists = take(X_PARTS), take(X_PARTS)
    left_rows, here_rows, there_rows, r_map, o_map, todo, sems = take(7)
    acc, chosen = (acc_out, chosen_out) if last else take(2)
    n_out, bs = pairs.shape[0], left.shape[-1]
    place, column = lax.axis_index("loop") % 4, lax.axis_index("bcast")
    mark = slot * n_x if last and chooses else 0

    half = n_left // 2
    margins = []
    for q, (lo, n) in enumerate(((0, half), (half, n_left - half))):
        source = left.at[pl.ds((slot * n_left + lo) * bs, n * bs)]
        margins.append(pltpu.make_async_copy(source, left_rows.at[pl.ds(lo * bs, n * bs)], sems.at[q]))
    if adds:
        sums_copy = pltpu.make_async_copy(acc_before, acc, sems.at[2])
        chosen_copy = pltpu.make_async_copy(chosen_before, chosen.at[pl.ds(0, mark)], sems.at[3])

    def fetch(at, parts, rows, lists):
        copies, entry = [], 0
        for p, array in enumerate(parts):
            right = arrays[array]
            n = right.shape[0] // bs
            target = rows.at[pl.ds(entry * bs, n * bs)]
            entry += n
            copies.append(pltpu.make_async_copy(right.at[pl.ds(0, n * bs)], target, sems.at[at + 2 * p]))
            listed = right.at[pl.ds(n * bs, LIST_ROWS)]
            copies.append(pltpu.make_async_copy(listed, lists[p], sems.at[at + 2 * p + 1]))
        return copies

    def copies_of(parts, here):
        if here:
            return fetch(7, parts, here_rows, here_lists)
        return fetch(7 + 2 * X_PARTS, parts, there_rows, there_lists)

    def place_in(lists, parts):
        at = [(p, j) for p, array in enumerate(parts) for j in range(arrays[array].shape[0] // bs)]
        return lambda j, d: lists[at[j][0]][0, 2 * at[j][1] + d].astype(jnp.int32)

    def each(then):
        for step, places, parts in plan:
            applies = functools.reduce(jnp.logical_or, [place == value for value in places])
            mine = owner[step] == column if chooses else True
            pl.when(applies & mine)(functools.partial(then, parts, True))
            if chooses:
                pl.when(applies & jnp.logical_not(mine))(functools.partial(then, parts, False))

    def start(wanted, parts, here):
        if here == wanted:
            for copy in copies_of(parts, here):
                copy.start()

    def land(wanted, parts, here):
        if here != wanted:
            return
        for copy in copies_of(parts, here):
            copy.wait()
        if here:
            fill_map(r_map, KB * CB, place_in(here_lists, parts), n_x, CB)
            return
        read = place_in(there_lists, parts)
        for j in range(n_x):
            for d in range(2):
                chosen_list[2 * (slot * n_x + j) + d] = read(j, d)

    def left_place(i):
        return left_list[slot * n_left + i, 0], left_list[slot * n_left + i, 1] * CB

    margins[0].start()
    each(functools.partial(start, True))
    if adds:
        sums_copy.start()
    margins[1].start()
    fill_map(o_map, RB * CB, lambda m, d: pairs[m, d], n_out, CB)
    if adds:
        for q in range(2 * slot * n_x):
            chosen_list[q] = list_before[q]
    else:
        acc[...] = jnp.zeros_like(acc)
    each(functools.partial(land, True))
    if adds:
        sums_copy.wait()
        chosen_copy.start()
    if chooses:
        each(functools.partial(start, False))
    arrivals = [(half, margins[0].wait), (n_left - half, margins[1].wait)]
    add_products(
        acc, n_out, bs, (r_map, o_map), todo, left_place, n_left, left_rows, lambda j: halves(block(here_rows, j, bs)), arrivals
    )
    if adds:
        chosen_copy.wait()
    if not chooses:
        return
    out_copies = []
    if not last:
        out_copies.append(pltpu.make_async_copy(acc, acc_out, sems.at[4]))
        out_copies[0].start()
    each(functools.partial(land, False))

    def split(j, carry):
        chosen[mark + j, 0], chosen[mark + j, 1] = halves(block(there_rows, j, bs))
        return carry

    for q, (lo, hi) in enumerate(((0, n_x // 2), (n_x // 2, n_x))):
        lax.fori_loop(lo, hi, split, 0)
        if not last:
            rows = pl.ds(lo, hi - lo)
            out_copies.append(pltpu.make_async_copy(chosen.at[rows], chosen_out.at[rows], sems.at[5 + q]))
            out_copies[-1].start()
    for copy in out_copies:
        copy.wait()


def own_products(owner, pairs, left, slot, left_list, n_left, choices, before, chooses, last):
    bs, n_out = left.shape[-1], pairs.shape[0]
    arrays, plan = [], []
    for step, places, parts in choices:
        at = []
        for part in parts:
            known = [i for i, other in enumerate(arrays) if other is part]
            if not known:
                known = [len(arrays)]
                arrays.append(part)
            at.append(known[0])
        plan.append((step, places, at))
    n_x = sum(part.shape[0] // bs for part in choices[0][2])
    anywhere = pl.BlockSpec(memory_space=pl.ANY)
    smem = [owner, pairs, left_list]
    operands = [pltpu.with_memory_space_constraint(rows, pltpu.HBM) for rows in (left, *arrays)]
    if before is not None:
        smem.append(before[2])
        operands += [pltpu.with_memory_space_constraint(one, pltpu.HBM) for one in before[:2]]
    acc_shape, chosen_shape = (n_out + 1, bs, bs), ((slot + 1) * n_x, 2, bs, bs)
    kind = pltpu.VMEM if last else pltpu.HBM
    out_shape, out_specs = [kind(acc_shape, jnp.float32)], [pl.BlockSpec(memory_space=kind)]
    if chooses:
        out_shape += [kind(chosen_shape, jnp.bfloat16), jax.ShapeDtypeStruct((2 * (slot + 1) * n_x,), jnp.int32)]
        out_specs += [pl.BlockSpec(memory_space=kind), SMEM]
    scratch = [pltpu.SMEM((LIST_ROWS, bs), jnp.float32)] * (2 * X_PARTS) + [
        pltpu.VMEM((n_left * bs, bs), jnp.float32),
        pltpu.VMEM((n_x * bs, bs), jnp.float32),
        pltpu.VMEM((n_x * bs, bs), jnp.float32),
        pltpu.SMEM(((KB + 1) * CB,), jnp.int32),
        pltpu.SMEM((RB * CB,), jnp.int32),
        pltpu.SMEM((n_left * CB + 4,), jnp.int32),
        pltpu.SemaphoreType.DMA((7 + 4 * X_PARTS,)),
    ]
    if not last:
        scratch += [pltpu.VMEM(acc_shape, jnp.float32), pltpu.VMEM(chosen_shape, jnp.bfloat16)]
    return pl.pallas_call(
        functools.partial(own_kernel, slot, n_left, n_x, plan, len(arrays), chooses, last),
        in_specs=[SMEM] * len(smem) + [anywhere] * len(operands),
        out_specs=out_specs,
        out_shape=out_shape,
        scratch_shapes=scratch,
        compiler_params=pltpu.CompilerParams(vmem_limit_bytes=OWN_LIMIT),
        cost_estimate=pl.CostEstimate(flops=0, bytes_accessed=2**20, transcendentals=0),
        name="own_products",
    )(*smem, *operands)


OWN_LIMIT = 24 * 2**20
LAST_LIMIT = 24 * 2**20


def last_kernel(n_s, pairs, late, right_list, left, before, chosen, out, acc, left_rows, maps, todo, sems):
    r_map, o_map, l_map = maps
    n_out, bs = pairs.shape[0], left.shape[-1]
    n_right, n_left = chosen.shape[0], left.shape[0] // bs
    depth = n_left // n_s
    n_x = n_right // depth
    starts = list(range(0, n_left, FETCH))
    fetched = []
    for q, lo in enumerate(starts):
        rows = pl.ds(lo * bs, min(FETCH, n_left - lo) * bs)
        fetched.append(pltpu.make_async_copy(left.at[rows], left_rows.at[rows], sems.at[n_out + q]))
    fetched[0].start()
    fill_map(o_map, RB * CB, lambda m, d: pairs[m, d], n_out, CB)
    for cell in range(r_map.shape[0]):
        r_map[cell] = -1
    for j in range(n_right):
        r_map[(j // n_x * (KB + 1) + right_list[2 * j]) * CB + right_list[2 * j + 1]] = j
    for m in range(n_out):
        acc[m] = before[m]
    fetched[1].start()

    def note(count, i, j, m):
        todo[count] = (i * 64 + jnp.maximum(j, 0)) * 64 + jnp.maximum(m, 0)
        return count + ((i >= 0) & (j >= 0) & (m >= 0)).astype(jnp.int32)

    def collect(i, count):
        row, base = late[2 * i], (i // n_s * (KB + 1) + late[2 * i + 1]) * CB
        for c in range(CB):
            count = note(count, i, r_map[base + c], o_map[row * CB + c])
        return count

    count, ends = jnp.int32(0), []
    for lo, hi in zip(starts, starts[1:]):
        count = lax.fori_loop(lo, hi, collect, count)
        ends.append(count // WIDE)
    ordered = count
    slots = range(starts[-1] // n_s, depth)
    for cell in range(l_map.shape[0]):
        l_map[cell] = -1
    for i in range(starts[-1], n_left):
        l_map[(i // n_s - slots[0]) * RB * KB + late[2 * i] * KB + late[2 * i + 1]] = i

    def gather(m, count):
        row, c = pairs[m, 0], pairs[m, 1]
        for slot in slots:
            for k in range(KB):
                i = l_map[(slot - slots[0]) * RB * KB + row * KB + k]
                count = note(count, i, r_map[(slot * (KB + 1) + k) * CB + c], m)
        return count

    count = lax.fori_loop(0, n_out, gather, count)
    for u in range(2 * NARROW):
        todo[count + u] = n_out

    def product(code):
        i, j, m = code // 4096, (code // 64) % 64, code % 64
        left_high, left_low = halves(block(left_rows, i, bs))
        high, low = chosen[j, 0], chosen[j, 1]
        for z in range(0, bs, bs // 2):
            part = slice(z, z + bs // 2)
            first, second = left_high[part], left_low[part]
            acc[m, part] += dot(first, high) + dot(first, low) + dot(second, high)

    def several(q, carry):
        for u in range(WIDE):
            product(todo[q * WIDE + u])
        return carry

    def send(m, carry):
        pltpu.make_async_copy(acc.at[m], out.at[m], sems.at[m]).start()
        return carry

    def several_and_send(q, sent):
        for u in range(NARROW):
            product(todo[q * NARROW + u])
        following = (q + 1) * NARROW
        done = jnp.where(following >= ordered, todo[following] % 64, sent)
        lax.fori_loop(sent, done, send, 0)
        return done

    at = 0
    for copy, end in zip(fetched, ends):
        copy.wait()
        if copy is fetched[0]:
            for later in fetched[2:]:
                later.start()
        lax.fori_loop(at, end, several, 0)
        at = end
    fetched[-1].wait()
    sent = lax.fori_loop(at * (WIDE // NARROW), (count + NARROW - 1) // NARROW, several_and_send, jnp.int32(0))
    lax.fori_loop(sent, n_out, send, 0)
    for m in range(n_out):
        pltpu.make_async_copy(acc.at[m], out.at[m], sems.at[m]).wait()


def last_products(pairs, late, left, n_s, acc, chosen, right_list):
    bs = left.shape[-1]
    n_out, depth = pairs.shape[0], left.shape[0] // (n_s * bs)
    anywhere = pl.BlockSpec(memory_space=pl.ANY)
    return pl.pallas_call(
        functools.partial(last_kernel, n_s),
        in_specs=[SMEM] * 3 + [anywhere] + [VMEM] * 2,
        out_specs=anywhere,
        out_shape=jax.ShapeDtypeStruct((n_out, bs, bs), jnp.float32),
        scratch_shapes=[
            pltpu.VMEM(acc.shape, acc.dtype),
            pltpu.VMEM(left.shape, left.dtype),
            [pltpu.SMEM((size,), jnp.int32) for size in (depth * (KB + 1) * CB, RB * CB, depth * RB * KB)],
            pltpu.SMEM((depth * n_s * CB + 2 * NARROW,), jnp.int32),
            pltpu.SemaphoreType.DMA((n_out + pl.cdiv(depth * n_s, FETCH),)),
        ],
        compiler_params=pltpu.CompilerParams(vmem_limit_bytes=LAST_LIMIT),
        cost_estimate=pl.CostEstimate(flops=0, bytes_accessed=2**20, transcendentals=0),
        name="last_products",
    )(pairs, late, right_list, pltpu.with_memory_space_constraint(left, pltpu.HBM), acc, chosen)


def per_device(s_blocks, s_list, x_blocks, x_list, c_list, owner):
    length, width = lax.axis_size("loop"), lax.axis_size("bcast")
    pairs, owner = c_list[0, 0], owner[0]
    depth, n_s, bs = s_blocks.shape[2], s_blocks.shape[3], s_blocks.shape[-1]
    n_x = x_blocks.shape[2]
    s_own, x_own = s_blocks.reshape(depth * n_s * bs, bs), x_blocks.reshape(n_x * bs, bs)
    s_own_list, x_own_list = s_list.reshape(depth * n_s, 2), x_list[0, 0]

    swapped = width == 2
    if swapped:
        partner = [(0, 1), (1, 0)]
        came = lax.ppermute(s_own, "bcast", partner)
        their_list = lax.ppermute(s_own_list.reshape(-1), "bcast", partner)
    else:
        held = lax.all_gather(s_own, "bcast")
        held_lists = lax.all_gather(s_own_list, "bcast")

    everything, *parts = pack(x_own, x_own_list)

    def moved(packed, to):
        return [lax.ppermute(part, "loop", [(g, (g + to[g % 4]) % length) for g in range(length)]) for part in packed]

    first = moved(parts, (-1, 1, -1, -3))
    second = moved(first, (1, -1, -3, -1))
    other = moved([everything], (-3, -1, -3, -1))

    choices = [(0, (0, 1, 2, 3), [everything]), (1, (1, 3), first), (1, (0, 2), other)]
    choices += [(2, (0, 1, 2, 3), second), (3, (0,), first), (3, (1, 3), other)]

    def last_choice():
        return (3, (2,), [lax.ppermute(part, "loop", [(g, g - 1) for g in range(3, length, 4)]) for part in second])

    if not swapped:
        choices.append(last_choice())
        total = 0
        for step in range(STEPS):
            piece = lax.dynamic_index_in_dim(held, owner[step], 0, False)
            places = lax.dynamic_index_in_dim(held_lists, owner[step], 0, False)
            fit = [choice for choice in choices if choice[0] == step]
            added = own_products(owner, pairs, piece, step // width, places, n_s, fit, None, False, True)
            total = total + added[0]
        return total[None, None, : pairs.shape[0]]

    sums = None
    for slot in range(depth):
        if slot == 1:
            second[-1], places = lax.optimization_barrier((second[-1], sums[2]))
            sums = (*sums[:2], places)
            choices.append(last_choice())
        fit = [choice for choice in choices if choice[0] // width == slot]
        sums = own_products(owner, pairs, s_own, slot, s_own_list, n_s, fit, sums, True, slot == depth - 1)
    return last_products(pairs, their_list, came, n_s, *sums)[None, None]


def solution(mesh):
    return jax.shard_map(
        per_device,
        mesh=mesh,
        in_specs=(
            P("loop", "bcast", None, None, None, None),
            P("loop", "bcast", None, None, None),
            P("loop", "bcast", None, None, None),
            P("loop", "bcast", None, None),
            P("loop", "bcast", None, None),
            P("loop", None),
        ),
        out_specs=P("loop", "bcast", None, None, None),
        check_vma=False,
    )
```
